512 devices in a mesh: lat: 2 (over core), lon: 8 (over y), mem: 32 (over z, x).
Axes of the slice: x: 4, y: 8, z: 8, core: 2. Of those that a mesh axis runs over, the one named last changes fastest.
Arguments:
- alpha: float32 [128, 64, 16, 1024], P(None, 'mem', 'lat', 'lon'), may hold values from -4 to 7
- perturb: bfloat16 [128, 64, 16, 1024], P(None, 'mem', 'lat', 'lon'), may hold values from -6 to 6
- smooth_gain: float32 [16, 1024], replicated, may hold values from 0.25 to 1
- bands: int32 [128], replicated, may hold values from 1 to 8, as said below
- steps: int32 [128], replicated, may hold values from 1 to 24, as said below
Outputs:
- increment: float32 [128, 16, 1024], P('mem', 'lat', 'lon')
The draws below stay inside these ranges and needn't reach their ends.
Inputs may be any that keep to these rules, and one draw needn't show every extreme that they name: `bands`: 8 is reached at some level. `steps`: 24 is reached at some level.
All inputs are finite; a program needn't handle non-finite values.
Results may differ from the reference program's by a relative error of at most 0.0003.
Values may be sent and summed in bfloat16 or wider, within the bound.
A program may use at most 64 MiB of HBM per device.

```python
import math
import jax
import jax.numpy as jnp
from jax import lax

LEV = 128
TLON = 128
STEPS_MAX = 24
BAND_MAX = 8
NLAT = 16
NLON = 1024
MEMBERS = 64


def edge_distance():
    columns = jnp.arange(NLON, dtype=jnp.int32) % TLON
    return jnp.minimum(columns, TLON - 1 - columns)


def draw_alpha(key, part):
    key = jax.random.fold_in(key, 31)
    shape = (LEV, MEMBERS, NLAT, NLON)
    distance = edge_distance()
    inside = ((distance >= STEPS_MAX // 3) & (distance < STEPS_MAX)).astype(jnp.float32)
    rough = jnp.clip(jax.random.normal(key, shape, jnp.float32), -4.0, 4.0)
    front = 3.0 * inside
    return (rough + front[None, None, None, :]).astype(jnp.float32)


def draw_smooth_gain(key, part):
    key = jax.random.fold_in(key, 41)
    distance = edge_distance()
    near_edge = (distance < STEPS_MAX)[None, :]
    lowest = 0.6
    far_gain = jnp.exp(jax.random.uniform(key, (NLAT, NLON), jnp.float32, jnp.log(0.25), 0.0))
    near_gain = jnp.exp(jax.random.uniform(jax.random.fold_in(key, 3), (NLAT, NLON), jnp.float32, jnp.log(lowest), 0.0))
    return jnp.clip(jnp.where(near_edge, near_gain, far_gain), 0.25, 1.0).astype(jnp.float32)


def draw_bands(key, part):
    key = jax.random.fold_in(key, 11)
    widths = jax.random.randint(key, (LEV,), 1, BAND_MAX + 1)
    picked = jax.random.randint(jax.random.fold_in(key, 5), (), 0, LEV)
    return widths.at[picked].set(BAND_MAX).astype(jnp.int32)


def draw_steps(key, part):
    key = jax.random.fold_in(key, 23)
    level_rows = jnp.arange(LEV, dtype=jnp.int32)
    upper = 2 + (STEPS_MAX - 1) * (level_rows + 1) // LEV
    counts = jax.random.randint(key, (LEV,), 1, upper)
    picked = LEV // 2 + jax.random.randint(jax.random.fold_in(key, 9), (4,), 0, LEV // 2)
    return counts.at[picked].set(STEPS_MAX).astype(jnp.int32)


def level_of(key, dims, split, smallest, high):
    level = 1.0
    for dim, blocks in split:
        steps = jax.random.uniform(jax.random.fold_in(jax.random.fold_in(key, 6), dim), (blocks,), jnp.float32, smallest / len(split), high / len(split))
        level = level * jnp.repeat(jnp.exp(steps), dims[dim] // blocks).reshape((-1,) + (1,) * (len(dims) - 1 - dim))
    return level


def scatter_about(rng, extent, scale, bound, cuts=(), held_as=jnp.bfloat16):
    level = level_of(rng, extent, cuts, -0.22, 0.18) if cuts else 1.0
    values = jax.random.normal(rng, extent, jnp.float32) * scale * level
    return jnp.minimum(jnp.maximum(values, -bound), bound).astype(held_as)


def setup_inputs(seed: int = 0) -> dict:
    key_of = jax.random.split(jax.random.key(seed), 6)
    return {
        "alpha": draw_alpha(jax.random.fold_in(key_of[5], 71), 0),
        "perturb": scatter_about(key_of[1], (LEV, MEMBERS, NLAT, NLON), 1.0, 6.0, ((1, 32), (2, 2), (3, 8))),
        "smooth_gain": draw_smooth_gain(jax.random.fold_in(key_of[5], 71), 0),
        "bands": draw_bands(jax.random.fold_in(key_of[5], 71), 0),
        "steps": draw_steps(jax.random.fold_in(key_of[5], 71), 0),
    }


def band_weights(bands):
    level_rows = jnp.arange(LEV, dtype=jnp.int32)
    distance = jnp.abs(level_rows[:, None] - level_rows[None, :]).astype(jnp.float32)
    band_width = bands.astype(jnp.float32)[:, None]
    raw_weights = jnp.where(distance <= band_width, 1.0 - distance / (band_width + 1.0), 0.0).astype(jnp.float32)
    return raw_weights / lax.optimization_barrier(jnp.sum(raw_weights, axis=1, keepdims=True))

def diffuse(values_in, coefficient, step_count):

    def one_step(step_index, state_now):
        padded = jnp.pad(state_now, ((0, 0), (1, 1), (1, 1)), mode='edge')
        beside_all = padded[:, 2:, 1:-1] + padded[:, :-2, 1:-1] + padded[:, 1:-1, 2:] + padded[:, 1:-1, :-2]
        return state_now + coefficient * (beside_all - 4.0 * state_now)
    return lax.fori_loop(0, step_count, one_step, values_in)

def reference(alpha, perturb, smooth_gain, bands, steps):
    weights = band_weights(bands)
    flattened = alpha.reshape(LEV, -1)
    vertical = jnp.dot(weights, flattened, precision=lax.Precision.HIGHEST, preferred_element_type=jnp.float32).reshape(alpha.shape)
    coefficient = 0.24 * smooth_gain
    member_scale = 1.0 / math.sqrt(MEMBERS)

    def level_work(inputs):
        field_level, perturb_level, step_count = inputs
        smoothed = diffuse(field_level, coefficient, step_count)
        return lax.optimization_barrier(jnp.sum(perturb_level.astype(jnp.float32) * smoothed, axis=0)) * member_scale
    return lax.map(level_work, (vertical, perturb, steps))
```

```python
import jax
import jax.numpy as jnp
from jax import lax
from jax.experimental import pallas as pl
from jax.experimental.pallas import tpu as pltpu
from jax.sharding import PartitionSpec as P

F32 = jnp.float32
BF16 = jnp.bfloat16
HALO = 24
TILE = 128
EXT = TILE + 2 * HALO
NJ = EXT // 8
ROWS = 16
MAX_STEPS = 24
NX = 4
NZ = 8
LON = 8


def iota(shape, dim):
    return lax.broadcasted_iota(jnp.int32, shape, dim)


def split2(value):
    high = value.astype(BF16)
    low = (value - high.astype(F32)).astype(BF16)
    return high, low


def dot(a, b):
    return jnp.dot(a, b, preferred_element_type=F32)


def diffuse_step(src, dst, cf, af, active, lclamp, rclamp, block):
    def body(b, carry):
        y0 = b * block
        above = jnp.maximum(y0 - 1, 0)
        below = jnp.minimum(y0 + block, ROWS - 1)
        ys = [y0 + i for i in range(block)]

        def load(y, j):
            return src[y, j * 8 : (j + 1) * 8, :]

        left = [pltpu.roll(load(y, NJ - 1), 1, 0) for y in ys]
        here = [load(y, 0) for y in ys]
        for j in range(NJ):
            if j < NJ - 1:
                right = [load(y, j + 1) for y in ys]
            else:
                right = [pltpu.roll(load(y, 0), 7, 0) for y in ys]
            column = [load(above, j)] + here + [load(below, j)]
            for i, y in enumerate(ys):
                a, c = left[i], right[i]
                if j == HALO % NJ:
                    a = jnp.where(lclamp, here[i], a)
                if j == (HALO + TILE - 1) % NJ:
                    c = jnp.where(rclamp, here[i], c)
                beside = (a + c) + (column[i] + column[i + 2])
                new = af[y, j * 8 : (j + 1) * 8, :] * here[i] + cf[y, j * 8 : (j + 1) * 8, :] * beside
                dst[y, j * 8 : (j + 1) * 8, :] = jnp.where(active, new, here[i])
            left, here = here, right
        return carry

    lax.fori_loop(0, ROWS // block, body, 0)


def kernel(
    alpha_ref, perturb_ref, gain_ref, bands_ref, steps_ref, out_ref,
    whi, wlo, vext, sib, ub0, ub1, cf, af, gt, pf, pt, psend, smo, xs, xr, acc, zs, zr,
    hs_sem, hr_sem, ps_sem, pr_sem, xs_sem, xr_sem, zs_sem, zr_sem,
):
    h = lax.axis_index("lat")
    g = lax.axis_index("lon")
    mi = lax.axis_index("mem")
    z = mi // NX
    x = mi % NX
    oh = 1 - h
    gl = lax.rem(g + LON - 1, LON)
    gr = lax.rem(g + 1, LON)

    def xmem(d):
        return z * NX + lax.rem(x + d, NX)

    def zmem(d):
        return lax.rem(z + d, NZ) * NX + x

    partners = [(oh, g, mi)]
    partners += [(a, b, mi) for a in (h, oh) for b in (gl, gr)]
    partners += [(h, g, xmem(d)) for d in range(1, NX)]
    partners += [(a, g, zmem(d)) for a in (h, oh) for d in range(1, NZ)]
    barrier = pltpu.get_barrier_semaphore()
    for p in partners:
        pl.semaphore_signal(barrier, inc=1, device_id=p, device_id_type=pl.DeviceIdType.MESH)

    def remote(src, dst, ssem, rsem, dev):
        return pltpu.make_async_remote_copy(
            src_ref=src, dst_ref=dst, send_sem=ssem, recv_sem=rsem,
            device_id=dev, device_id_type=pl.DeviceIdType.MESH,
        )

    n = iota((128, 256), 1)
    k = iota((128, 256), 0)
    core = lax.rem(h + n // 128, 2)
    member = lax.rem(n // 64, 2)
    q = lax.rem(n, 64)
    level = lax.rem(q, 8) * 16 + (q // 16) * 4 + core * 2 + lax.rem(q // 8, 2)
    onehot = jnp.where(k == level, 1.0, 0.0).astype(BF16)
    r8 = iota((8, 128), 0)
    rows = jnp.where(
        r8 == 0,
        jnp.broadcast_to(bands_ref[...].astype(F32), (8, 128)),
        jnp.broadcast_to(steps_ref[...].astype(F32), (8, 128)),
    ).astype(BF16)
    permuted = dot(rows, onehot)
    width = jnp.broadcast_to(permuted[0:1, :], (128, 256))
    count = jnp.broadcast_to(permuted[1:2, 0:128], (8, 128))
    distance = jnp.abs(k - level).astype(F32)
    raw = jnp.where(distance <= width, 1.0 - distance / (width + 1.0), 0.0)
    weights = raw / jnp.sum(raw, axis=0, keepdims=True)
    for m in range(2):
        high, low = split2(jnp.where(member == m, weights, 0.0))
        whi[m * 128 : (m + 1) * 128, :] = high
        wlo[m * 128 : (m + 1) * 128, :] = low

    def vertical(y, carry):
        a0 = alpha_ref[pl.ds(y, 128, stride=16), :]
        a1 = alpha_ref[pl.ds(y + 8, 128, stride=16), :]
        high, low = split2(jnp.concatenate([a0.T, a1.T], axis=1))
        w = whi[...]
        v = dot(high, w) + dot(low, w) + dot(high, wlo[...])
        vext[h * 8 + y, HALO : HALO + TILE, :] = v[:, 0:128]
        sib[y] = v[:, 128:256]
        return carry

    halo_copies = []
    for b in range(2):
        lax.fori_loop(4 * b, 4 * b + 4, vertical, 0)
        if b == 0:
            pl.semaphore_wait(barrier, len(partners))
        own_rows = pl.ds(h * 8 + 4 * b, 4)
        sib_rows = pl.ds(4 * b, 4)
        lefts = pl.ds(0, HALO)
        rights = pl.ds(HALO + TILE, HALO)
        sends = [
            (vext.at[own_rows, pl.ds(HALO, HALO)], vext.at[own_rows, rights], (h, gl, mi)),
            (vext.at[own_rows, pl.ds(TILE, HALO)], vext.at[own_rows, lefts], (h, gr, mi)),
            (sib.at[sib_rows, pl.ds(0, HALO)], vext.at[own_rows, rights], (oh, gl, mi)),
            (sib.at[sib_rows, pl.ds(TILE - HALO, HALO)], vext.at[own_rows, lefts], (oh, gr, mi)),
            (sib.at[sib_rows], vext.at[own_rows, pl.ds(HALO, TILE)], (oh, g, mi)),
        ]
        for i, (src, dst, dev) in enumerate(sends):
            cp = remote(src, dst, hs_sem.at[b, i], hr_sem.at[b, i], dev)
            cp.start()
            halo_copies.append(cp)

    def widen(i, carry):
        at = pl.ds(pl.multiple_of(i * 256, 256), 256)
        pf[at, :] = perturb_ref[at, :].astype(F32)
        return carry

    lax.fori_loop(0, 8, widen, 0)

    def pick(y, c):
        parts = []
        for m in range(2):
            for xx in range(NX):
                for lv in range(2):
                    parts.append(pf[pl.ds(xx * 64 + c * 32 + lv * 16 + m * 8 + y, 8, stride=256), :])
        return jnp.concatenate(parts, axis=0).astype(BF16)

    def pick_other(y, carry):
        psend[y] = pick(y, oh)
        return carry

    def pick_own(y, carry):
        pt[h * 8 + y] = pick(y, h)
        return carry

    lax.fori_loop(0, 8, pick_other, 0)
    pcopy = remote(psend, pt.at[pl.ds(h * 8, 8)], ps_sem.at[0], pr_sem.at[0], (oh, g, mi))
    pcopy.start()
    lax.fori_loop(0, 8, pick_own, 0)

    def gain_tile(t):
        tile = gain_ref[:, pl.ds(pl.multiple_of(t * TILE, TILE), TILE)]
        return (0.24 * jnp.concatenate([tile, jnp.zeros((TILE - ROWS, TILE), F32)], axis=0)).T

    gt[0:HALO, :] = gain_tile(gl)[TILE - HALO :, :]
    gt[HALO : HALO + TILE, :] = gain_tile(g)
    gt[HALO + TILE :, :] = gain_tile(gr)[:HALO, :]
    gp = jnp.concatenate([gt[pl.ds(j, 8, stride=NJ), :] for j in range(NJ)], axis=0)
    g1 = gp.astype(BF16).astype(F32)
    g2 = (gp - g1).astype(BF16).astype(F32)
    g3 = gp - g1 - g2
    gsplit = (g1 + pltpu.roll(g2, 16, 1) + pltpu.roll(g3, 32, 1)).astype(BF16)
    rr = iota((128, 128), 0)

    def spread(y, carry):
        pickrow = jnp.where(jnp.logical_and(rr < 48, lax.rem(rr, 16) == y), 1.0, 0.0).astype(BF16)
        c = dot(gsplit, pickrow)
        cf[y] = c
        af[y] = 1.0 - 4.0 * c
        return carry

    lax.fori_loop(0, ROWS, spread, 0)

    for cp in halo_copies:
        cp.wait_recv()

    def restride(y, carry):
        for j in range(NJ):
            ub0[y, j * 8 : (j + 1) * 8, :] = vext[y, pl.ds(j, 8, stride=NJ), :]
        return carry

    lax.fori_loop(0, ROWS, restride, 0)

    sub = iota((8, 128), 0)
    lclamp = jnp.logical_and(sub == HALO // NJ, g == 0)
    rclamp = jnp.logical_and(sub == (HALO + TILE - 1) // NJ, g == LON - 1)

    def two_steps(s, carry):
        t = (2 * s).astype(F32)
        diffuse_step(ub0, ub1, cf, af, t < count, lclamp, rclamp, 8)
        diffuse_step(ub1, ub0, cf, af, t + 1.0 < count, lclamp, rclamp, 8)
        return carry

    lax.fori_loop(0, MAX_STEPS // 2, two_steps, 0)

    pcopy.wait_recv()

    def weigh(y, carry):
        for j in range(NJ):
            smo[pl.ds(j, 8, stride=NJ), :] = ub0[y, j * 8 : (j + 1) * 8, :]
        product = smo[HALO : HALO + TILE, :].T * pt[y].astype(F32)
        total = (product[0:64, :] + product[64:128, :]) * 0.125
        for xx in range(NX):
            xs[xx, y] = total[xx * 16 : (xx + 1) * 16, :]
        return carry

    xcopies = []
    for b in range(2):
        lax.fori_loop(8 * b, 8 * b + 8, weigh, 0)
        half = pl.ds(8 * b, 8)
        for d in range(1, NX):
            cp = remote(
                xs.at[lax.rem(x + d, NX), half], xr.at[d - 1, half],
                xs_sem.at[b, d - 1], xr_sem.at[b, d - 1], (h, g, xmem(d)),
            )
            cp.start()
            xcopies.append(cp)

    for cp in xcopies:
        cp.wait_recv()

    def gather(y, carry):
        acc[pl.ds(pl.multiple_of(y * 16, 16), 16), :] = (xs[x, y] + xr[0, y]) + (xr[1, y] + xr[2, y])
        return carry

    lax.fori_loop(0, ROWS, gather, 0)

    for zz in range(NZ):
        for hh in range(2):
            for lv in range(2):
                zs[zz, hh, lv] = acc[pl.ds(hh * 128 + lv * 8 + zz, 8, stride=16), :]

    zcopies = []
    for d in range(NZ):
        for e in range(2):
            if d == 0 and e == 0:
                continue
            cp = remote(
                zs.at[lax.rem(z + d, NZ), lax.rem(h + e, 2)], zr.at[d * 2 + e],
                zs_sem.at[d * 2 + e], zr_sem.at[d * 2 + e], (lax.rem(h + e, 2), g, zmem(d)),
            )
            cp.start()
            zcopies.append(cp)
    for cp in zcopies:
        cp.wait_recv()
    same = zs[z, h]
    other = zr[1]
    for d in range(1, NZ):
        same = same + zr[2 * d]
        other = other + zr[2 * d + 1]
    out_ref[pl.ds(2 * h, 2)] = same
    out_ref[pl.ds(2 * oh, 2)] = other

    for cp in halo_copies + [pcopy] + xcopies + zcopies:
        cp.wait_send()


def body(alpha, perturb, smooth_gain, bands, steps):
    vmem = pl.BlockSpec(memory_space=pltpu.VMEM)
    dma = pltpu.SemaphoreType.DMA
    return pl.pallas_call(
        kernel,
        out_shape=jax.ShapeDtypeStruct((4, 8, TILE), F32),
        in_specs=[vmem] * 5,
        out_specs=vmem,
        scratch_shapes=[
            pltpu.VMEM((256, 256), BF16),
            pltpu.VMEM((256, 256), BF16),
            pltpu.VMEM((ROWS, EXT, 128), F32),
            pltpu.VMEM((8, TILE, 128), F32),
            pltpu.VMEM((ROWS, EXT, 128), F32),
            pltpu.VMEM((ROWS, EXT, 128), F32),
            pltpu.VMEM((ROWS, EXT, 128), F32),
            pltpu.VMEM((ROWS, EXT, 128), F32),
            pltpu.VMEM((EXT, 128), F32),
            pltpu.VMEM((2048, 128), F32),
            pltpu.VMEM((ROWS, 128, TILE), BF16),
            pltpu.VMEM((8, 128, TILE), BF16),
            pltpu.VMEM((EXT, 128), F32),
            pltpu.VMEM((NX, ROWS, 16, TILE), F32),
            pltpu.VMEM((NX - 1, ROWS, 16, TILE), F32),
            pltpu.VMEM((256, TILE), F32),
            pltpu.VMEM((NZ, 2, 2, 8, TILE), F32),
            pltpu.VMEM((2 * NZ, 2, 8, TILE), F32),
            dma((2, 5)), dma((2, 5)), dma((1,)), dma((1,)),
            dma((2, 3)), dma((2, 3)), dma((16,)), dma((16,)),
        ],
        compiler_params=pltpu.CompilerParams(
            collective_id=0, has_side_effects=True, vmem_limit_bytes=48 << 20
        ),
    )(
        alpha.reshape(2048, TILE),
        perturb.reshape(2048, TILE),
        smooth_gain,
        bands.reshape(1, 128),
        steps.reshape(1, 128),
    )


def solution(mesh):
    placed = (P(None, "mem", "lat", "lon"), P(None, "mem", "lat", "lon"), P(), P(), P())
    return jax.shard_map(
        body, mesh=mesh, in_specs=placed, out_specs=P("mem", "lat", "lon"), check_vma=False
    )
```

```python
import jax
import jax.numpy as jnp
from jax import lax
from jax.experimental import pallas as pl
from jax.experimental.pallas import tpu as pltpu
from jax.sharding import PartitionSpec as P

F32 = jnp.float32
BF16 = jnp.bfloat16
HALO = 24
TILE = 128
EXT = TILE + 2 * HALO
NJ = EXT // 8
ROWS = 16
MAX_STEPS = 24
NX = 4
NZ = 8
LON = 8


def iota(shape, dim):
    return lax.broadcasted_iota(jnp.int32, shape, dim)


def split2(value):
    high = value.astype(BF16)
    low = (value - high.astype(F32)).astype(BF16)
    return high, low


def dot(a, b):
    return jnp.dot(a, b, preferred_element_type=F32)


def diffuse_step(src, dst, cf, af, active, lclamp, rclamp, block):
    def body(b, carry):
        y0 = b * block
        above = jnp.maximum(y0 - 1, 0)
        below = jnp.minimum(y0 + block, ROWS - 1)
        ys = [y0 + i for i in range(block)]

        def load(y, j):
            return src[y, j * 8 : (j + 1) * 8, :]

        left = [pltpu.roll(load(y, NJ - 1), 1, 0) for y in ys]
        here = [load(y, 0) for y in ys]
        pairs = None
        for j in range(NJ):
            if j < NJ - 1:
                right = [load(y, j + 1) for y in ys]
            else:
                right = [pltpu.roll(load(y, 0), 7, 0) for y in ys]
            top, bottom = load(above, j), load(below, j)
            if j == HALO % NJ:
                left = [jnp.where(lclamp, u, a) for u, a in zip(here, left)]
            if pairs is None or j == HALO % NJ:
                up_left = [u + a for u, a in zip([top] + here[:-1], left)]
            else:
                up_left = [top + left[0]] + pairs[:-1]
            beyond = right
            if j == (HALO + TILE - 1) % NJ:
                beyond = [jnp.where(rclamp, u, a) for u, a in zip(here, right)]
            pairs = [d + r for d, r in zip(here[1:] + [bottom], beyond)]
            for i, y in enumerate(ys):
                at = (y, slice(j * 8, (j + 1) * 8), slice(None))
                new = af[at] * here[i] + cf[at] * (up_left[i] + pairs[i])
                dst[at] = jnp.where(active, new, here[i])
            left, here = here, right
        return carry

    lax.fori_loop(0, ROWS // block, body, 0)


def kernel(
    alpha_hbm, perturb_hbm, gain_hbm, bands_hbm, steps_hbm, out_ref,
    alpha_ref, perturb_ref, gain_ref, bands_ref, steps_ref,
    whi, wlo, vext, sib, hsend, hrecv, ub0, ub1, cf, af, gt, pf, pt, psend, smo, xs, xr, acc, zs, zr,
    in_sem, hs_sem, hr_sem, ps_sem, pr_sem, xs_sem, xr_sem, zs_sem, zr_sem,
):
    h = lax.axis_index("lat")
    g = lax.axis_index("lon")
    mi = lax.axis_index("mem")
    z = mi // NX
    x = mi % NX
    oh = 1 - h
    gl = lax.rem(g + LON - 1, LON)
    gr = lax.rem(g + 1, LON)

    def xmem(d):
        return z * NX + lax.rem(x + d, NX)

    def zmem(d):
        return lax.rem(z + d, NZ) * NX + x

    partners = [(oh, g, mi)]
    partners += [(a, b, mi) for a in (h, oh) for b in (gl, gr)]
    partners += [(h, g, xmem(d)) for d in range(1, NX)]
    partners += [(a, g, zmem(d)) for a in (h, oh) for d in range(1, NZ)]
    barrier = pltpu.get_barrier_semaphore()
    for p in partners:
        pl.semaphore_signal(barrier, inc=1, device_id=p, device_id_type=pl.DeviceIdType.MESH)

    loads = [
        pltpu.make_async_copy(bands_hbm, bands_ref, in_sem.at[0]),
        pltpu.make_async_copy(steps_hbm, steps_ref, in_sem.at[1]),
    ]
    for i in range(4):
        part = pl.ds(i * 512, 512)
        loads.append(pltpu.make_async_copy(alpha_hbm.at[part], alpha_ref.at[part], in_sem.at[2 + i]))
    loads.append(pltpu.make_async_copy(gain_hbm, gain_ref, in_sem.at[6]))
    loads.append(pltpu.make_async_copy(perturb_hbm, perturb_ref, in_sem.at[7]))
    for cp in loads:
        cp.start()

    def remote(src, dst, ssem, rsem, dev):
        return pltpu.make_async_remote_copy(
            src_ref=src, dst_ref=dst, send_sem=ssem, recv_sem=rsem,
            device_id=dev, device_id_type=pl.DeviceIdType.MESH,
        )

    loads[0].wait()
    loads[1].wait()
    n = iota((128, 256), 1)
    k = iota((128, 256), 0)
    core = lax.rem(h + n // 128, 2)
    member = lax.rem(n // 64, 2)
    q = lax.rem(n, 64)
    level = lax.rem(q, 8) * 16 + (q // 16) * 4 + core * 2 + lax.rem(q // 8, 2)
    onehot = jnp.where(k == level, 1.0, 0.0).astype(BF16)
    r8 = iota((8, 128), 0)
    rows = jnp.where(
        r8 == 0,
        jnp.broadcast_to(bands_ref[...].astype(F32), (8, 128)),
        jnp.broadcast_to(steps_ref[...].astype(F32), (8, 128)),
    ).astype(BF16)
    permuted = dot(rows, onehot)
    width = jnp.broadcast_to(permuted[0:1, :], (128, 256))
    count = jnp.broadcast_to(permuted[1:2, 0:128], (8, 128))
    distance = jnp.abs(k - level).astype(F32)
    raw = jnp.where(distance <= width, 1.0 - distance / (width + 1.0), 0.0)
    weights = raw / jnp.sum(raw, axis=0, keepdims=True)
    for m in range(2):
        high, low = split2(jnp.where(member == m, weights, 0.0))
        whi[m * 128 : (m + 1) * 128, :] = high
        wlo[m * 128 : (m + 1) * 128, :] = low

    def vertical(p, carry):
        turned = []
        for i in range(2):
            y = 2 * p + i
            a0 = alpha_ref[pl.ds(y, 128, stride=16), :]
            a1 = alpha_ref[pl.ds(y + 8, 128, stride=16), :]
            turned.append(jnp.concatenate([a0.T, a1.T], axis=1))
        high, low = split2(jnp.concatenate(turned, axis=0))
        w = whi[...]
        v = dot(high, w) + dot(low, w) + dot(high, wlo[...])
        for i in range(2):
            vext[h * 8 + 2 * p + i, HALO : HALO + TILE, :] = v[i * TILE : (i + 1) * TILE, 0:128]
            sib[2 * p + i] = v[i * TILE : (i + 1) * TILE, 128:256]
        for core in range(2):
            c = v[:, core * 128 : (core + 1) * 128]
            for side, x0 in enumerate((0, TILE - HALO)):
                hsend[core, side, p] = jnp.concatenate(
                    [c[x0 : x0 + HALO], c[TILE + x0 : TILE + x0 + HALO]], axis=0
                ).astype(BF16)
        return carry

    for cp in loads[2:6]:
        cp.wait()
    halo_copies = []
    for b in range(2):
        lax.fori_loop(2 * b, 2 * b + 2, vertical, 0)
        if b == 0:
            pl.semaphore_wait(barrier, len(partners))
        own_pairs = pl.ds(h * 4 + 2 * b, 2)
        pairs = pl.ds(2 * b, 2)
        sends = [
            (hsend.at[0, 0, pairs], hrecv.at[1, own_pairs], (h, gl, mi)),
            (hsend.at[0, 1, pairs], hrecv.at[0, own_pairs], (h, gr, mi)),
            (hsend.at[1, 0, pairs], hrecv.at[1, own_pairs], (oh, gl, mi)),
            (hsend.at[1, 1, pairs], hrecv.at[0, own_pairs], (oh, gr, mi)),
            (sib.at[pl.ds(4 * b, 4)], vext.at[pl.ds(h * 8 + 4 * b, 4), pl.ds(HALO, TILE)], (oh, g, mi)),
        ]
        for i, (src, dst, dev) in enumerate(sends):
            cp = remote(src, dst, hs_sem.at[b, i], hr_sem.at[b, i], dev)
            cp.start()
            halo_copies.append(cp)

    def widen(i, carry):
        at = pl.ds(pl.multiple_of(i * 256, 256), 256)
        pf[at, :] = perturb_ref[at, :].astype(F32)
        return carry

    loads[7].wait()
    lax.fori_loop(0, 8, widen, 0)

    def pick(y, c):
        parts = []
        for m in range(2):
            for xx in range(NX):
                for lv in range(2):
                    parts.append(pf[pl.ds(xx * 64 + c * 32 + lv * 16 + m * 8 + y, 8, stride=256), :])
        return jnp.concatenate(parts, axis=0).astype(BF16)

    def pick_other(y, carry):
        psend[y] = pick(y, oh)
        return carry

    def pick_own(y, carry):
        pt[h * 8 + y] = pick(y, h)
        return carry

    lax.fori_loop(0, 8, pick_other, 0)
    pcopy = remote(psend, pt.at[pl.ds(h * 8, 8)], ps_sem.at[0], pr_sem.at[0], (oh, g, mi))
    pcopy.start()
    lax.fori_loop(0, 8, pick_own, 0)

    loads[6].wait()
    def gain_tile(t):
        tile = gain_ref[:, pl.ds(pl.multiple_of(t * TILE, TILE), TILE)]
        return (0.24 * jnp.concatenate([tile, jnp.zeros((TILE - ROWS, TILE), F32)], axis=0)).T

    gt[0:HALO, :] = gain_tile(gl)[TILE - HALO :, :]
    gt[HALO : HALO + TILE, :] = gain_tile(g)
    gt[HALO + TILE :, :] = gain_tile(gr)[:HALO, :]

    def spread(j, carry):
        columns = gt[pl.ds(j, 8, stride=NJ), :]
        at = pl.ds(pl.multiple_of(j * 8, 8), 8)
        for y in range(ROWS):
            c = jnp.broadcast_to(columns[:, y : y + 1], (8, 128))
            cf[y, at, :] = c
            af[y, at, :] = 1.0 - 4.0 * c
        return carry

    lax.fori_loop(0, NJ, spread, 0)

    for cp in halo_copies:
        cp.wait_recv()

    def restride(p, carry):
        lefts = hrecv[0, p].astype(F32)
        rights = hrecv[1, p].astype(F32)
        for i in range(2):
            y = 2 * p + i
            vext[y, 0:HALO, :] = lefts[i * HALO : (i + 1) * HALO]
            vext[y, HALO + TILE :, :] = rights[i * HALO : (i + 1) * HALO]
            for j in range(NJ):
                ub0[y, j * 8 : (j + 1) * 8, :] = vext[y, pl.ds(j, 8, stride=NJ), :]
        return carry

    lax.fori_loop(0, ROWS // 2, restride, 0)

    sub = iota((8, 128), 0)
    lclamp = jnp.logical_and(sub == HALO // NJ, g == 0)
    rclamp = jnp.logical_and(sub == (HALO + TILE - 1) // NJ, g == LON - 1)

    def two_steps(s, carry):
        t = (2 * s).astype(F32)
        diffuse_step(ub0, ub1, cf, af, t < count, lclamp, rclamp, 8)
        diffuse_step(ub1, ub0, cf, af, t + 1.0 < count, lclamp, rclamp, 8)
        return carry

    lax.fori_loop(0, MAX_STEPS // 2, two_steps, 0)

    pcopy.wait_recv()

    def weigh(i, base):
        for k in range(4):
            y = base + 4 * i + k
            for j in range(NJ):
                smo[k, pl.ds(j, 8, stride=NJ), :] = ub0[y, j * 8 : (j + 1) * 8, :]
        for k in range(4):
            y = base + 4 * i + k
            product = smo[k, HALO : HALO + TILE, :].T * pt[y].astype(F32)
            total = (product[0:64, :] + product[64:128, :]) * 0.125
            for xx in range(NX):
                xs[xx, y] = total[xx * 16 : (xx + 1) * 16, :]
        return base

    xcopies = []
    for e in (1, 0):
        base = 8 * lax.rem(h + e, 2)
        lax.fori_loop(0, 2, weigh, base)
        half = pl.ds(base, 8)
        group = []
        for d in range(1, NX):
            cp = remote(
                xs.at[lax.rem(x + d, NX), half], xr.at[d - 1, half],
                xs_sem.at[e, d - 1], xr_sem.at[e, d - 1], (h, g, xmem(d)),
            )
            cp.start()
            group.append(cp)
        xcopies.append(group)

    zcopies = []
    for e, group in zip((1, 0), xcopies):
        to = lax.rem(h + e, 2)
        base = 8 * to
        for cp in group:
            cp.wait_recv()

        def gather(i, carry):
            y = base + i
            acc[pl.ds(pl.multiple_of(y * 16, 16), 16), :] = (xs[x, y] + xr[0, y]) + (xr[1, y] + xr[2, y])
            return carry

        lax.fori_loop(0, 8, gather, 0)
        for zz in range(NZ):
            for lv in range(2):
                zs[zz, e, lv] = acc[pl.ds(to * 128 + lv * 8 + zz, 8, stride=16), :]
        for d in range(NZ):
            if d == 0 and e == 0:
                continue
            cp = remote(
                zs.at[lax.rem(z + d, NZ), e], zr.at[d * 2 + e],
                zs_sem.at[d * 2 + e], zr_sem.at[d * 2 + e], (to, g, zmem(d)),
            )
            cp.start()
            zcopies.append(cp)
    for cp in zcopies:
        cp.wait_recv()
    same = zs[z, 0]
    other = zr[1]
    for d in range(1, NZ):
        same = same + zr[2 * d]
        other = other + zr[2 * d + 1]
    out_ref[pl.ds(2 * h, 2)] = same
    out_ref[pl.ds(2 * oh, 2)] = other

    for cp in halo_copies + [pcopy] + xcopies[0] + xcopies[1] + zcopies:
        cp.wait_send()


def body(alpha, perturb, smooth_gain, bands, steps):
    vmem = pl.BlockSpec(memory_space=pltpu.VMEM)
    dma = pltpu.SemaphoreType.DMA
    return pl.pallas_call(
        kernel,
        out_shape=jax.ShapeDtypeStruct((4, 8, TILE), F32),
        in_specs=[pl.BlockSpec(memory_space=pl.ANY)] * 5,
        out_specs=vmem,
        scratch_shapes=[
            pltpu.VMEM((2048, TILE), F32),
            pltpu.VMEM((2048, TILE), BF16),
            pltpu.VMEM((ROWS, LON * TILE), F32),
            pltpu.VMEM((1, 128), jnp.int32),
            pltpu.VMEM((1, 128), jnp.int32),
            pltpu.VMEM((256, 256), BF16),
            pltpu.VMEM((256, 256), BF16),
            pltpu.VMEM((ROWS, EXT, 128), F32),
            pltpu.VMEM((8, TILE, 128), F32),
            pltpu.VMEM((2, 2, 4, 2 * HALO, 128), BF16),
            pltpu.VMEM((2, ROWS // 2, 2 * HALO, 128), BF16),
            pltpu.VMEM((ROWS, EXT, 128), F32),
            pltpu.VMEM((ROWS, EXT, 128), F32),
            pltpu.VMEM((ROWS, EXT, 128), F32),
            pltpu.VMEM((ROWS, EXT, 128), F32),
            pltpu.VMEM((EXT, 128), F32),
            pltpu.VMEM((2048, 128), F32),
            pltpu.VMEM((ROWS, 128, TILE), BF16),
            pltpu.VMEM((8, 128, TILE), BF16),
            pltpu.VMEM((4, EXT, 128), F32),
            pltpu.VMEM((NX, ROWS, 16, TILE), F32),
            pltpu.VMEM((NX - 1, ROWS, 16, TILE), F32),
            pltpu.VMEM((256, TILE), F32),
            pltpu.VMEM((NZ, 2, 2, 8, TILE), F32),
            pltpu.VMEM((2 * NZ, 2, 8, TILE), F32),
            dma((8,)), dma((2, 5)), dma((2, 5)), dma((1,)), dma((1,)),
            dma((2, 3)), dma((2, 3)), dma((16,)), dma((16,)),
        ],
        compiler_params=pltpu.CompilerParams(
            collective_id=0, has_side_effects=True, vmem_limit_bytes=60 << 20
        ),
    )(
        alpha.reshape(2048, TILE),
        perturb.reshape(2048, TILE),
        smooth_gain,
        bands.reshape(1, 128),
        steps.reshape(1, 128),
    )


def solution(mesh):
    placed = (P(None, "mem", "lat", "lon"), P(None, "mem", "lat", "lon"), P(), P(), P())
    return jax.shard_map(
        body, mesh=mesh, in_specs=placed, out_specs=P("mem", "lat", "lon"), check_vma=False
    )
```

```python
import jax
import jax.numpy as jnp
from jax import lax
from jax.experimental import pallas as pl
from jax.experimental.pallas import tpu as pltpu
from jax.sharding import PartitionSpec as P

F32 = jnp.float32
BF16 = jnp.bfloat16
HALO = 24
TILE = 128
EXT = TILE + 2 * HALO
NJ = EXT // 8
ROWS = 16
MAX_STEPS = 24
NX = 4
NZ = 8
LON = 8


def iota(shape, dim):
    return lax.broadcasted_iota(jnp.int32, shape, dim)


def split2(value):
    high = value.astype(BF16)
    low = (value - high.astype(F32)).astype(BF16)
    return high, low


def dot(a, b):
    return jnp.dot(a, b, preferred_element_type=F32)


def diffuse_step(src, dst, cf, af, active, lclamp, rclamp, block):
    def body(b, carry):
        y0 = b * block
        above = jnp.maximum(y0 - 1, 0)
        below = jnp.minimum(y0 + block, ROWS - 1)
        ys = [y0 + i for i in range(block)]

        def load(y, j):
            return src[y, j * 8 : (j + 1) * 8, :]

        left = [pltpu.roll(load(y, NJ - 1), 1, 0) for y in ys]
        here = [load(y, 0) for y in ys]
        pairs = None
        for j in range(NJ):
            if j < NJ - 1:
                right = [load(y, j + 1) for y in ys]
            else:
                right = [pltpu.roll(load(y, 0), 7, 0) for y in ys]
            top, bottom = load(above, j), load(below, j)
            if j == HALO % NJ:
                left = [jnp.where(lclamp, u, a) for u, a in zip(here, left)]
            if pairs is None or j == HALO % NJ:
                up_left = [u + a for u, a in zip([top] + here[:-1], left)]
            else:
                up_left = [top + left[0]] + pairs[:-1]
            beyond = right
            if j == (HALO + TILE - 1) % NJ:
                beyond = [jnp.where(rclamp, u, a) for u, a in zip(here, right)]
            pairs = [d + r for d, r in zip(here[1:] + [bottom], beyond)]
            for i, y in enumerate(ys):
                at = (y, slice(j * 8, (j + 1) * 8), slice(None))
                new = af[at] * here[i] + cf[at] * (up_left[i] + pairs[i])
                dst[at] = jnp.where(active, new, here[i])
            left, here = here, right
        return carry

    lax.fori_loop(0, ROWS // block, body, 0)


def kernel(
    alpha_hbm, perturb_hbm, gain_hbm, bands_hbm, steps_hbm, out_ref,
    alpha_ref, perturb_ref, gain_ref, bands_ref, steps_ref,
    whi, wlo, vext, sib, hsend, hrecv, ub0, ub1, cf, af, gt, pf, pt, psend, smo, xs, xq, xscale, xr, xrscale, acc, zs, zr,
    in_sem, hs_sem, hr_sem, ps_sem, pr_sem, xs_sem, xr_sem, zs_sem, zr_sem,
):
    h = lax.axis_index("lat")
    g = lax.axis_index("lon")
    mi = lax.axis_index("mem")
    z = mi // NX
    x = mi % NX
    oh = 1 - h
    gl = lax.rem(g + LON - 1, LON)
    gr = lax.rem(g + 1, LON)

    def xmem(d):
        return z * NX + lax.rem(x + d, NX)

    def zmem(d):
        return lax.rem(z + d, NZ) * NX + x

    partners = [(oh, g, mi)]
    partners += [(a, b, mi) for a in (h, oh) for b in (gl, gr)]
    partners += [(h, g, xmem(d)) for d in range(1, NX)]
    partners += [(a, g, zmem(d)) for a in (h, oh) for d in range(1, NZ)]
    barrier = pltpu.get_barrier_semaphore()
    for p in partners:
        pl.semaphore_signal(barrier, inc=1, device_id=p, device_id_type=pl.DeviceIdType.MESH)

    loads = [
        pltpu.make_async_copy(bands_hbm, bands_ref, in_sem.at[0]),
        pltpu.make_async_copy(steps_hbm, steps_ref, in_sem.at[1]),
    ]
    for i in range(4):
        part = pl.ds(i * 512, 512)
        loads.append(pltpu.make_async_copy(alpha_hbm.at[part], alpha_ref.at[part], in_sem.at[2 + i]))
    loads.append(pltpu.make_async_copy(gain_hbm, gain_ref, in_sem.at[6]))
    loads.append(pltpu.make_async_copy(perturb_hbm, perturb_ref, in_sem.at[7]))
    for cp in loads:
        cp.start()

    def remote(src, dst, ssem, rsem, dev):
        return pltpu.make_async_remote_copy(
            src_ref=src, dst_ref=dst, send_sem=ssem, recv_sem=rsem,
            device_id=dev, device_id_type=pl.DeviceIdType.MESH,
        )

    loads[0].wait()
    loads[1].wait()
    n = iota((128, 256), 1)
    k = iota((128, 256), 0)
    core = lax.rem(h + n // 128, 2)
    member = lax.rem(n // 64, 2)
    q = lax.rem(n, 64)
    level = lax.rem(q, 8) * 16 + (q // 16) * 4 + core * 2 + lax.rem(q // 8, 2)
    onehot = jnp.where(k == level, 1.0, 0.0).astype(BF16)
    r8 = iota((8, 128), 0)
    rows = jnp.where(
        r8 == 0,
        jnp.broadcast_to(bands_ref[...].astype(F32), (8, 128)),
        jnp.broadcast_to(steps_ref[...].astype(F32), (8, 128)),
    ).astype(BF16)
    permuted = dot(rows, onehot)
    width = jnp.broadcast_to(permuted[0:1, :], (128, 256))
    count = jnp.broadcast_to(permuted[1:2, 0:128], (8, 128))
    distance = jnp.abs(k - level).astype(F32)
    raw = jnp.where(distance <= width, 1.0 - distance / (width + 1.0), 0.0)
    weights = raw / jnp.sum(raw, axis=0, keepdims=True)
    for m in range(2):
        high, low = split2(jnp.where(member == m, weights, 0.0))
        whi[m * 128 : (m + 1) * 128, :] = high
        wlo[m * 128 : (m + 1) * 128, :] = low

    def vertical(p, carry):
        turned = []
        for i in range(2):
            y = 2 * p + i
            a0 = alpha_ref[pl.ds(y, 128, stride=16), :]
            a1 = alpha_ref[pl.ds(y + 8, 128, stride=16), :]
            turned.append(jnp.concatenate([a0.T, a1.T], axis=1))
        high, low = split2(jnp.concatenate(turned, axis=0))
        w = whi[...]
        v = dot(high, w) + dot(low, w) + dot(high, wlo[...])
        for i in range(2):
            vext[h * 8 + 2 * p + i, HALO : HALO + TILE, :] = v[i * TILE : (i + 1) * TILE, 0:128]
            sib[2 * p + i] = v[i * TILE : (i + 1) * TILE, 128:256]
        for core in range(2):
            c = v[:, core * 128 : (core + 1) * 128]
            for side, x0 in enumerate((0, TILE - HALO)):
                hsend[core, side, p] = jnp.concatenate(
                    [c[x0 : x0 + HALO], c[TILE + x0 : TILE + x0 + HALO]], axis=0
                ).astype(BF16)
        return carry

    for cp in loads[2:6]:
        cp.wait()
    lax.fori_loop(0, 4, vertical, 0)
    pl.semaphore_wait(barrier, len(partners))
    own_pairs = pl.ds(h * 4, 4)
    sends = [
        (hsend.at[0, 0], hrecv.at[1, own_pairs], (h, gl, mi)),
        (hsend.at[0, 1], hrecv.at[0, own_pairs], (h, gr, mi)),
        (hsend.at[1, 0], hrecv.at[1, own_pairs], (oh, gl, mi)),
        (hsend.at[1, 1], hrecv.at[0, own_pairs], (oh, gr, mi)),
        (sib, vext.at[pl.ds(h * 8, 8), pl.ds(HALO, TILE)], (oh, g, mi)),
    ]
    halo_copies = []
    for i, (src, dst, dev) in enumerate(sends):
        cp = remote(src, dst, hs_sem.at[i], hr_sem.at[i], dev)
        cp.start()
        halo_copies.append(cp)

    def widen(i, carry):
        at = pl.ds(pl.multiple_of(i * 256, 256), 256)
        pf[at, :] = perturb_ref[at, :].astype(F32)
        return carry

    loads[7].wait()
    lax.fori_loop(0, 8, widen, 0)

    def pick(y, c):
        parts = []
        for m in range(2):
            for xx in range(NX):
                for lv in range(2):
                    parts.append(pf[pl.ds(xx * 64 + c * 32 + lv * 16 + m * 8 + y, 8, stride=256), :])
        return jnp.concatenate(parts, axis=0).astype(BF16)

    def pick_other(y, carry):
        psend[y] = pick(y, oh)
        return carry

    def pick_own(y, carry):
        pt[h * 8 + y] = pick(y, h)
        return carry

    lax.fori_loop(0, 8, pick_other, 0)
    pcopy = remote(psend, pt.at[pl.ds(h * 8, 8)], ps_sem.at[0], pr_sem.at[0], (oh, g, mi))
    pcopy.start()
    lax.fori_loop(0, 8, pick_own, 0)

    loads[6].wait()
    def gain_tile(t):
        tile = gain_ref[:, pl.ds(pl.multiple_of(t * TILE, TILE), TILE)]
        return (0.24 * jnp.concatenate([tile, jnp.zeros((TILE - ROWS, TILE), F32)], axis=0)).T

    gt[0:HALO, :] = gain_tile(gl)[TILE - HALO :, :]
    gt[HALO : HALO + TILE, :] = gain_tile(g)
    gt[HALO + TILE :, :] = gain_tile(gr)[:HALO, :]

    def spread(j, carry):
        columns = gt[pl.ds(j, 8, stride=NJ), :]
        at = pl.ds(pl.multiple_of(j * 8, 8), 8)
        for y in range(ROWS):
            c = jnp.broadcast_to(columns[:, y : y + 1], (8, 128))
            cf[y, at, :] = c
            af[y, at, :] = 1.0 - 4.0 * c
        return carry

    lax.fori_loop(0, NJ, spread, 0)

    for cp in halo_copies:
        cp.wait_recv()

    def restride(p, carry):
        lefts = hrecv[0, p].astype(F32)
        rights = hrecv[1, p].astype(F32)
        for i in range(2):
            y = 2 * p + i
            vext[y, 0:HALO, :] = lefts[i * HALO : (i + 1) * HALO]
            vext[y, HALO + TILE :, :] = rights[i * HALO : (i + 1) * HALO]
            for j in range(NJ):
                ub0[y, j * 8 : (j + 1) * 8, :] = vext[y, pl.ds(j, 8, stride=NJ), :]
        return carry

    lax.fori_loop(0, ROWS // 2, restride, 0)

    sub = iota((8, 128), 0)
    lclamp = jnp.logical_and(sub == HALO // NJ, g == 0)
    rclamp = jnp.logical_and(sub == (HALO + TILE - 1) // NJ, g == LON - 1)

    def two_steps(s, carry):
        t = (2 * s).astype(F32)
        diffuse_step(ub0, ub1, cf, af, t < count, lclamp, rclamp, 8)
        diffuse_step(ub1, ub0, cf, af, t + 1.0 < count, lclamp, rclamp, 8)
        return carry

    lax.fori_loop(0, MAX_STEPS // 2, two_steps, 0)

    pcopy.wait_recv()

    def weigh(i, base):
        for k in range(4):
            y = base + 4 * i + k
            for j in range(NJ):
                smo[k, pl.ds(j, 8, stride=NJ), :] = ub0[y, j * 8 : (j + 1) * 8, :]
        for k in range(4):
            y = base + 4 * i + k
            product = smo[k, HALO : HALO + TILE, :].T * pt[y].astype(F32)
            total = (product[0:64, :] + product[64:128, :]) * 0.125
            for xx in range(NX):
                part = total[xx * 16 : (xx + 1) * 16, :]
                xs[xx, y] = part
                peak = jnp.max(jnp.abs(part), axis=0, keepdims=True)
                inverse = jnp.where(peak > 1e-30, 32767.0 / jnp.maximum(peak, 1e-30), 0.0)
                xq[xx, y] = jnp.round(part * inverse).astype(jnp.int32).astype(jnp.int16)
                xscale[xx, pl.ds(y, 1), :] = peak * (1.0 / 32767.0)
        return base

    xcopies = []
    for e in (1, 0):
        base = 8 * lax.rem(h + e, 2)
        lax.fori_loop(0, 2, weigh, base)
        half = pl.ds(base, 8)
        group = []
        for d in (2, 1, 3):
            to = lax.rem(x + d, NX)
            for cp in (
                remote(
                    xq.at[to, half], xr.at[d - 1, half],
                    xs_sem.at[e, d - 1, 0], xr_sem.at[e, d - 1, 0], (h, g, xmem(d)),
                ),
                remote(
                    xscale.at[to, half], xrscale.at[d - 1, half],
                    xs_sem.at[e, d - 1, 1], xr_sem.at[e, d - 1, 1], (h, g, xmem(d)),
                ),
            ):
                cp.start()
                group.append(cp)
        xcopies.append(group)

    zcopies = []
    for e, group in zip((1, 0), xcopies):
        to = lax.rem(h + e, 2)
        base = 8 * to
        for cp in group:
            cp.wait_recv()

        def gather(i, carry):
            y = base + i
            total = xs[x, y]
            for d in range(NX - 1):
                total = total + xr[d, y].astype(jnp.int32).astype(F32) * xrscale[d, pl.ds(y, 1), :]
            acc[pl.ds(pl.multiple_of(y * 16, 16), 16), :] = total
            return carry

        lax.fori_loop(0, 8, gather, 0)
        for zz in range(NZ):
            for lv in range(2):
                zs[zz, e, lv] = acc[pl.ds(to * 128 + lv * 8 + zz, 8, stride=16), :]
        for d in (4, 3, 5, 2, 6, 1, 7, 0):
            if d == 0 and e == 0:
                continue
            cp = remote(
                zs.at[lax.rem(z + d, NZ), e], zr.at[d * 2 + e],
                zs_sem.at[d * 2 + e], zr_sem.at[d * 2 + e], (to, g, zmem(d)),
            )
            cp.start()
            zcopies.append(cp)
    for cp in zcopies:
        cp.wait_recv()
    same = zs[z, 0]
    other = zr[1]
    for d in range(1, NZ):
        same = same + zr[2 * d]
        other = other + zr[2 * d + 1]
    out_ref[pl.ds(2 * h, 2)] = same
    out_ref[pl.ds(2 * oh, 2)] = other

    for cp in halo_copies + [pcopy] + xcopies[0] + xcopies[1] + zcopies:
        cp.wait_send()


def body(alpha, perturb, smooth_gain, bands, steps):
    vmem = pl.BlockSpec(memory_space=pltpu.VMEM)
    dma = pltpu.SemaphoreType.DMA
    return pl.pallas_call(
        kernel,
        out_shape=jax.ShapeDtypeStruct((4, 8, TILE), F32),
        in_specs=[pl.BlockSpec(memory_space=pl.ANY)] * 5,
        out_specs=vmem,
        scratch_shapes=[
            pltpu.VMEM((2048, TILE), F32),
            pltpu.VMEM((2048, TILE), BF16),
            pltpu.VMEM((ROWS, LON * TILE), F32),
            pltpu.VMEM((1, 128), jnp.int32),
            pltpu.VMEM((1, 128), jnp.int32),
            pltpu.VMEM((256, 256), BF16),
            pltpu.VMEM((256, 256), BF16),
            pltpu.VMEM((ROWS, EXT, 128), F32),
            pltpu.VMEM((8, TILE, 128), F32),
            pltpu.VMEM((2, 2, 4, 2 * HALO, 128), BF16),
            pltpu.VMEM((2, ROWS // 2, 2 * HALO, 128), BF16),
            pltpu.VMEM((ROWS, EXT, 128), F32),
            pltpu.VMEM((ROWS, EXT, 128), F32),
            pltpu.VMEM((ROWS, EXT, 128), F32),
            pltpu.VMEM((ROWS, EXT, 128), F32),
            pltpu.VMEM((EXT, 128), F32),
            pltpu.VMEM((2048, 128), F32),
            pltpu.VMEM((ROWS, 128, TILE), BF16),
            pltpu.VMEM((8, 128, TILE), BF16),
            pltpu.VMEM((4, EXT, 128), F32),
            pltpu.VMEM((NX, ROWS, 16, TILE), F32),
            pltpu.VMEM((NX, ROWS, 16, TILE), jnp.int16),
            pltpu.VMEM((NX, ROWS, TILE), F32),
            pltpu.VMEM((NX - 1, ROWS, 16, TILE), jnp.int16),
            pltpu.VMEM((NX - 1, ROWS, TILE), F32),
            pltpu.VMEM((256, TILE), F32),
            pltpu.VMEM((NZ, 2, 2, 8, TILE), F32),
            pltpu.VMEM((2 * NZ, 2, 8, TILE), F32),
            dma((8,)), dma((5,)), dma((5,)), dma((1,)), dma((1,)),
            dma((2, 3, 2)), dma((2, 3, 2)), dma((16,)), dma((16,)),
        ],
        compiler_params=pltpu.CompilerParams(
            collective_id=0, has_side_effects=True, vmem_limit_bytes=60 << 20
        ),
    )(
        alpha.reshape(2048, TILE),
        perturb.reshape(2048, TILE),
        smooth_gain,
        bands.reshape(1, 128),
        steps.reshape(1, 128),
    )


def solution(mesh):
    placed = (P(None, "mem", "lat", "lon"), P(None, "mem", "lat", "lon"), P(), P(), P())
    return jax.shard_map(
        body, mesh=mesh, in_specs=placed, out_specs=P("mem", "lat", "lon"), check_vma=False
    )
```

```python
import jax
import jax.numpy as jnp
from jax import lax
from jax.experimental import pallas as pl
from jax.experimental.pallas import tpu as pltpu
from jax.sharding import PartitionSpec as P

F32 = jnp.float32
BF16 = jnp.bfloat16
HALO = 24
TILE = 128
EXT = TILE + 2 * HALO
NJ = EXT // 8
ROWS = 16
MAX_STEPS = 24
NX = 4
NZ = 8
LON = 8


def iota(shape, dim):
    return lax.broadcasted_iota(jnp.int32, shape, dim)


def split2(value):
    high = value.astype(BF16)
    low = (value - high.astype(F32)).astype(BF16)
    return high, low


def dot(a, b):
    return jnp.dot(a, b, preferred_element_type=F32)


def diffuse_step(src, dst, cf, af, active, lclamp, rclamp, block):
    def body(b, carry):
        y0 = b * block
        above = jnp.maximum(y0 - 1, 0)
        below = jnp.minimum(y0 + block, ROWS - 1)
        ys = [y0 + i for i in range(block)]

        def load(y, j):
            return src[y, j * 8 : (j + 1) * 8, :]

        left = [pltpu.roll(load(y, NJ - 1), 1, 0) for y in ys]
        here = [load(y, 0) for y in ys]
        pairs = None
        for j in range(NJ):
            if j < NJ - 1:
                right = [load(y, j + 1) for y in ys]
            else:
                right = [pltpu.roll(load(y, 0), 7, 0) for y in ys]
            top, bottom = load(above, j), load(below, j)
            if j == HALO % NJ:
                left = [jnp.where(lclamp, u, a) for u, a in zip(here, left)]
            if pairs is None or j == HALO % NJ:
                up_left = [u + a for u, a in zip([top] + here[:-1], left)]
            else:
                up_left = [top + left[0]] + pairs[:-1]
            beyond = right
            if j == (HALO + TILE - 1) % NJ:
                beyond = [jnp.where(rclamp, u, a) for u, a in zip(here, right)]
            pairs = [d + r for d, r in zip(here[1:] + [bottom], beyond)]
            for i, y in enumerate(ys):
                at = (y, slice(j * 8, (j + 1) * 8), slice(None))
                new = af[at] * here[i] + cf[at] * (up_left[i] + pairs[i])
                dst[at] = jnp.where(active, new, here[i])
            left, here = here, right
        return carry

    lax.fori_loop(0, ROWS // block, body, 0)


def kernel(
    alpha_hbm, perturb_hbm, gain_hbm, bands_hbm, steps_hbm, out_ref,
    alpha_ref, perturb_ref, gain_ref, bands_ref, steps_ref,
    whi, wlo, vext, sib, hsend, hrecv, ub0, ub1, cf, af, gt, pf, pt, psend, smo, xs, xq, xscale, xr, xrscale, acc, zs, zr,
    in_sem, relay, hs_sem, hr_sem, ps_sem, pr_sem, xs_sem, xr_sem, zs_sem, zr_sem,
):
    h = lax.axis_index("lat")
    g = lax.axis_index("lon")
    mi = lax.axis_index("mem")
    z = mi // NX
    x = mi % NX
    oh = 1 - h
    gl = lax.rem(g + LON - 1, LON)
    gr = lax.rem(g + 1, LON)

    def xmem(d):
        return z * NX + lax.rem(x + d, NX)

    def zmem(d):
        return lax.rem(z + d, NZ) * NX + x

    partners = [(oh, g, mi)]
    partners += [(a, b, mi) for a in (h, oh) for b in (gl, gr)]
    ring = [(h, g, zmem(1)), (h, g, zmem(NZ - 1)), (h, g, xmem(1)), (h, g, xmem(NX - 1))]
    partners += ring
    barrier = pltpu.get_barrier_semaphore()
    for p in partners:
        pl.semaphore_signal(barrier, inc=1, device_id=p, device_id_type=pl.DeviceIdType.MESH)

    loads = [
        pltpu.make_async_copy(bands_hbm, bands_ref, in_sem.at[0]),
        pltpu.make_async_copy(steps_hbm, steps_ref, in_sem.at[1]),
    ]
    for i in range(4):
        part = pl.ds(i * 512, 512)
        loads.append(pltpu.make_async_copy(alpha_hbm.at[part], alpha_ref.at[part], in_sem.at[2 + i]))
    loads.append(pltpu.make_async_copy(gain_hbm, gain_ref, in_sem.at[6]))
    loads.append(pltpu.make_async_copy(perturb_hbm, perturb_ref, in_sem.at[7]))
    for cp in loads:
        cp.start()

    def relay_send(r):
        for i in range(4 if r == 1 else 2):
            pl.semaphore_signal(
                relay.at[r - 1, i], inc=1, device_id=ring[i], device_id_type=pl.DeviceIdType.MESH
            )

    def relay_wait(r):
        for i in range(4 if r == 1 else 2):
            pl.semaphore_wait(relay.at[r - 1, i], 1)

    def remote(src, dst, ssem, rsem, dev):
        return pltpu.make_async_remote_copy(
            src_ref=src, dst_ref=dst, send_sem=ssem, recv_sem=rsem,
            device_id=dev, device_id_type=pl.DeviceIdType.MESH,
        )

    loads[0].wait()
    loads[1].wait()
    n = iota((128, 256), 1)
    k = iota((128, 256), 0)
    core = lax.rem(h + n // 128, 2)
    member = lax.rem(n // 64, 2)
    q = lax.rem(n, 64)
    level = lax.rem(q, 8) * 16 + (q // 16) * 4 + core * 2 + lax.rem(q // 8, 2)
    onehot = jnp.where(k == level, 1.0, 0.0).astype(BF16)
    r8 = iota((8, 128), 0)
    rows = jnp.where(
        r8 == 0,
        jnp.broadcast_to(bands_ref[...].astype(F32), (8, 128)),
        jnp.broadcast_to(steps_ref[...].astype(F32), (8, 128)),
    ).astype(BF16)
    permuted = dot(rows, onehot)
    width = jnp.broadcast_to(permuted[0:1, :], (128, 256))
    count = jnp.broadcast_to(permuted[1:2, 0:128], (8, 128))
    distance = jnp.abs(k - level).astype(F32)
    raw = jnp.where(distance <= width, 1.0 - distance / (width + 1.0), 0.0)
    weights = raw / jnp.sum(raw, axis=0, keepdims=True)
    for m in range(2):
        high, low = split2(jnp.where(member == m, weights, 0.0))
        whi[m * 128 : (m + 1) * 128, :] = high
        wlo[m * 128 : (m + 1) * 128, :] = low

    def vertical(p, carry):
        turned = []
        for i in range(2):
            y = 2 * p + i
            a0 = alpha_ref[pl.ds(y, 128, stride=16), :]
            a1 = alpha_ref[pl.ds(y + 8, 128, stride=16), :]
            turned.append(jnp.concatenate([a0.T, a1.T], axis=1))
        high, low = split2(jnp.concatenate(turned, axis=0))
        w = whi[...]
        v = dot(high, w) + dot(low, w) + dot(high, wlo[...])
        for i in range(2):
            vext[h * 8 + 2 * p + i, HALO : HALO + TILE, :] = v[i * TILE : (i + 1) * TILE, 0:128]
            sib[2 * p + i] = v[i * TILE : (i + 1) * TILE, 128:256]
        for core in range(2):
            c = v[:, core * 128 : (core + 1) * 128]
            for side, x0 in enumerate((0, TILE - HALO)):
                hsend[core, side, p] = jnp.concatenate(
                    [c[x0 : x0 + HALO], c[TILE + x0 : TILE + x0 + HALO]], axis=0
                ).astype(BF16)
        return carry

    for cp in loads[2:6]:
        cp.wait()
    halo_copies = []
    for b in range(2):
        lax.fori_loop(2 * b, 2 * b + 2, vertical, 0)
        if b == 0:
            pl.semaphore_wait(barrier, len(partners))
            relay_send(1)
        own_pairs = pl.ds(h * 4 + 2 * b, 2)
        pairs = pl.ds(2 * b, 2)
        sends = [
            (hsend.at[0, 0, pairs], hrecv.at[1, own_pairs], (h, gl, mi)),
            (hsend.at[0, 1, pairs], hrecv.at[0, own_pairs], (h, gr, mi)),
            (hsend.at[1, 0, pairs], hrecv.at[1, own_pairs], (oh, gl, mi)),
            (hsend.at[1, 1, pairs], hrecv.at[0, own_pairs], (oh, gr, mi)),
            (sib.at[pl.ds(4 * b, 4)], vext.at[pl.ds(h * 8 + 4 * b, 4), pl.ds(HALO, TILE)], (oh, g, mi)),
        ]
        for i, (src, dst, dev) in enumerate(sends):
            cp = remote(src, dst, hs_sem.at[b, i], hr_sem.at[b, i], dev)
            cp.start()
            halo_copies.append(cp)

    def widen(i, carry):
        at = pl.ds(pl.multiple_of(i * 256, 256), 256)
        pf[at, :] = perturb_ref[at, :].astype(F32)
        return carry

    loads[7].wait()
    lax.fori_loop(0, 8, widen, 0)

    def pick(y, c):
        parts = []
        for m in range(2):
            for xx in range(NX):
                for lv in range(2):
                    parts.append(pf[pl.ds(xx * 64 + c * 32 + lv * 16 + m * 8 + y, 8, stride=256), :])
        return jnp.concatenate(parts, axis=0).astype(BF16)

    def pick_other(y, carry):
        psend[y] = pick(y, oh)
        return carry

    def pick_own(y, carry):
        pt[h * 8 + y] = pick(y, h)
        return carry

    lax.fori_loop(0, 8, pick_other, 0)
    pcopy = remote(psend, pt.at[pl.ds(h * 8, 8)], ps_sem.at[0], pr_sem.at[0], (oh, g, mi))
    pcopy.start()
    lax.fori_loop(0, 8, pick_own, 0)

    loads[6].wait()
    def gain_tile(t):
        tile = gain_ref[:, pl.ds(pl.multiple_of(t * TILE, TILE), TILE)]
        return (0.24 * jnp.concatenate([tile, jnp.zeros((TILE - ROWS, TILE), F32)], axis=0)).T

    gt[0:HALO, :] = gain_tile(gl)[TILE - HALO :, :]
    gt[HALO : HALO + TILE, :] = gain_tile(g)
    gt[HALO + TILE :, :] = gain_tile(gr)[:HALO, :]

    def spread(i, carry):
        for k in range(2):
            j = 2 * i + k
            columns = gt[pl.ds(j, 8, stride=NJ), :]
            at = pl.ds(pl.multiple_of(j * 8, 8), 8)
            for y in range(ROWS):
                c = jnp.broadcast_to(columns[:, y : y + 1], (8, 128))
                cf[y, at, :] = c
                af[y, at, :] = 1.0 - 4.0 * c
        return carry

    lax.fori_loop(0, NJ // 2, spread, 0)

    relay_wait(1)
    relay_send(2)
    for cp in halo_copies:
        cp.wait_recv()

    def restride(p, carry):
        lefts = hrecv[0, p].astype(F32)
        rights = hrecv[1, p].astype(F32)
        for i in range(2):
            y = 2 * p + i
            vext[y, 0:HALO, :] = lefts[i * HALO : (i + 1) * HALO]
            vext[y, HALO + TILE :, :] = rights[i * HALO : (i + 1) * HALO]
            for j in range(NJ):
                ub0[y, j * 8 : (j + 1) * 8, :] = vext[y, pl.ds(j, 8, stride=NJ), :]
        return carry

    lax.fori_loop(0, ROWS // 2, restride, 0)

    relay_wait(2)
    relay_send(3)
    sub = iota((8, 128), 0)
    lclamp = jnp.logical_and(sub == HALO // NJ, g == 0)
    rclamp = jnp.logical_and(sub == (HALO + TILE - 1) // NJ, g == LON - 1)

    def two_steps(s, carry):
        t = (2 * s).astype(F32)
        diffuse_step(ub0, ub1, cf, af, t < count, lclamp, rclamp, 8)
        diffuse_step(ub1, ub0, cf, af, t + 1.0 < count, lclamp, rclamp, 8)
        return carry

    lax.fori_loop(0, MAX_STEPS // 4, two_steps, 0)
    relay_wait(3)
    relay_send(4)
    lax.fori_loop(MAX_STEPS // 4, MAX_STEPS // 2, two_steps, 0)
    relay_wait(4)

    pcopy.wait_recv()

    def weigh(i, base):
        for k in range(4):
            y = base + 4 * i + k
            for j in range(NJ):
                smo[k, pl.ds(j, 8, stride=NJ), :] = ub0[y, j * 8 : (j + 1) * 8, :]
        for k in range(4):
            y = base + 4 * i + k
            product = smo[k, HALO : HALO + TILE, :].T * pt[y].astype(F32)
            total = (product[0:64, :] + product[64:128, :]) * 0.125
            for xx in range(NX):
                part = total[xx * 16 : (xx + 1) * 16, :]
                xs[xx, y] = part
                peak = jnp.max(jnp.abs(part), axis=0, keepdims=True)
                inverse = jnp.where(peak > 1e-30, 32767.0 / jnp.maximum(peak, 1e-30), 0.0)
                xq[xx, y] = jnp.round(part * inverse).astype(jnp.int32).astype(jnp.int16)
                xscale[xx, pl.ds(y, 1), :] = peak * (1.0 / 32767.0)
        return base

    xcopies = []
    for e in (1, 0):
        base = 8 * lax.rem(h + e, 2)
        lax.fori_loop(0, 2, weigh, base)
        half = pl.ds(base, 8)
        group = []
        for d in (2, 1, 3):
            to = lax.rem(x + d, NX)
            for cp in (
                remote(
                    xq.at[to, half], xr.at[d - 1, half],
                    xs_sem.at[e, d - 1, 0], xr_sem.at[e, d - 1, 0], (h, g, xmem(d)),
                ),
                remote(
                    xscale.at[to, half], xrscale.at[d - 1, half],
                    xs_sem.at[e, d - 1, 1], xr_sem.at[e, d - 1, 1], (h, g, xmem(d)),
                ),
            ):
                cp.start()
                group.append(cp)
        xcopies.append(group)

    zcopies = []
    for e, group in zip((1, 0), xcopies):
        to = lax.rem(h + e, 2)
        base = 8 * to
        for cp in group:
            cp.wait_recv()

        def gather(i, carry):
            y = base + i
            total = xs[x, y]
            for d in range(NX - 1):
                total = total + xr[d, y].astype(jnp.int32).astype(F32) * xrscale[d, pl.ds(y, 1), :]
            acc[pl.ds(pl.multiple_of(y * 16, 16), 16), :] = total
            return carry

        lax.fori_loop(0, 8, gather, 0)
        for zz in range(NZ):
            for lv in range(2):
                zs[zz, e, lv] = acc[pl.ds(to * 128 + lv * 8 + zz, 8, stride=16), :]
        for d in (4, 3, 5, 2, 6, 1, 7, 0):
            if d == 0 and e == 0:
                continue
            cp = remote(
                zs.at[lax.rem(z + d, NZ), e], zr.at[d * 2 + e],
                zs_sem.at[d * 2 + e], zr_sem.at[d * 2 + e], (to, g, zmem(d)),
            )
            cp.start()
            zcopies.append(cp)
    for cp in zcopies:
        cp.wait_recv()
    same = zs[z, 0]
    other = zr[1]
    for d in range(1, NZ):
        same = same + zr[2 * d]
        other = other + zr[2 * d + 1]
    out_ref[pl.ds(2 * h, 2)] = same
    out_ref[pl.ds(2 * oh, 2)] = other

    for cp in halo_copies + [pcopy] + xcopies[0] + xcopies[1] + zcopies:
        cp.wait_send()


def body(alpha, perturb, smooth_gain, bands, steps):
    vmem = pl.BlockSpec(memory_space=pltpu.VMEM)
    dma = pltpu.SemaphoreType.DMA
    return pl.pallas_call(
        kernel,
        out_shape=jax.ShapeDtypeStruct((4, 8, TILE), F32),
        in_specs=[pl.BlockSpec(memory_space=pl.ANY)] * 5,
        out_specs=vmem,
        scratch_shapes=[
            pltpu.VMEM((2048, TILE), F32),
            pltpu.VMEM((2048, TILE), BF16),
            pltpu.VMEM((ROWS, LON * TILE), F32),
            pltpu.VMEM((1, 128), jnp.int32),
            pltpu.VMEM((1, 128), jnp.int32),
            pltpu.VMEM((256, 256), BF16),
            pltpu.VMEM((256, 256), BF16),
            pltpu.VMEM((ROWS, EXT, 128), F32),
            pltpu.VMEM((8, TILE, 128), F32),
            pltpu.VMEM((2, 2, 4, 2 * HALO, 128), BF16),
            pltpu.VMEM((2, ROWS // 2, 2 * HALO, 128), BF16),
            pltpu.VMEM((ROWS, EXT, 128), F32),
            pltpu.VMEM((ROWS, EXT, 128), F32),
            pltpu.VMEM((ROWS, EXT, 128), F32),
            pltpu.VMEM((ROWS, EXT, 128), F32),
            pltpu.VMEM((EXT, 128), F32),
            pltpu.VMEM((2048, 128), F32),
            pltpu.VMEM((ROWS, 128, TILE), BF16),
            pltpu.VMEM((8, 128, TILE), BF16),
            pltpu.VMEM((4, EXT, 128), F32),
            pltpu.VMEM((NX, ROWS, 16, TILE), F32),
            pltpu.VMEM((NX, ROWS, 16, TILE), jnp.int16),
            pltpu.VMEM((NX, ROWS, TILE), F32),
            pltpu.VMEM((NX - 1, ROWS, 16, TILE), jnp.int16),
            pltpu.VMEM((NX - 1, ROWS, TILE), F32),
            pltpu.VMEM((256, TILE), F32),
            pltpu.VMEM((NZ, 2, 2, 8, TILE), F32),
            pltpu.VMEM((2 * NZ, 2, 8, TILE), F32),
            dma((8,)), pltpu.SemaphoreType.REGULAR((4, 4)), dma((2, 5)), dma((2, 5)), dma((1,)), dma((1,)),
            dma((2, 3, 2)), dma((2, 3, 2)), dma((16,)), dma((16,)),
        ],
        compiler_params=pltpu.CompilerParams(
            collective_id=0, has_side_effects=True, vmem_limit_bytes=60 << 20
        ),
    )(
        alpha.reshape(2048, TILE),
        perturb.reshape(2048, TILE),
        smooth_gain,
        bands.reshape(1, 128),
        steps.reshape(1, 128),
    )


def solution(mesh):
    placed = (P(None, "mem", "lat", "lon"), P(None, "mem", "lat", "lon"), P(), P(), P())
    return jax.shard_map(
        body, mesh=mesh, in_specs=placed, out_specs=P("mem", "lat", "lon"), check_vma=False
    )
```

```python
import jax
import jax.numpy as jnp
from jax import lax
from jax.experimental import pallas as pl
from jax.experimental.pallas import tpu as pltpu
from jax.sharding import PartitionSpec as P

F32 = jnp.float32
BF16 = jnp.bfloat16
HALO = 24
TILE = 128
EXT = TILE + 2 * HALO
NJ = EXT // 8
ROWS = 16
MAX_STEPS = 24
NX = 4
NZ = 8
LON = 8


def iota(shape, dim):
    return lax.broadcasted_iota(jnp.int32, shape, dim)


def split2(value):
    high = value.astype(BF16)
    low = (value - high.astype(F32)).astype(BF16)
    return high, low


def dot(a, b):
    return jnp.dot(a, b, preferred_element_type=F32)


def diffuse_step(src, dst, cf, af, active, lclamp, rclamp, block):
    def body(b, carry):
        y0 = b * block
        above = jnp.maximum(y0 - 1, 0)
        below = jnp.minimum(y0 + block, ROWS - 1)
        ys = [y0 + i for i in range(block)]

        def load(y, j):
            return src[y, j * 8 : (j + 1) * 8, :]

        left = [pltpu.roll(load(y, NJ - 1), 1, 0) for y in ys]
        here = [load(y, 0) for y in ys]
        pairs = None
        for j in range(NJ):
            if j < NJ - 1:
                right = [load(y, j + 1) for y in ys]
            else:
                right = [pltpu.roll(load(y, 0), 7, 0) for y in ys]
            top, bottom = load(above, j), load(below, j)
            if j == HALO % NJ:
                left = [jnp.where(lclamp, u, a) for u, a in zip(here, left)]
            if pairs is None or j == HALO % NJ:
                up_left = [u + a for u, a in zip([top] + here[:-1], left)]
            else:
                up_left = [top + left[0]] + pairs[:-1]
            beyond = right
            if j == (HALO + TILE - 1) % NJ:
                beyond = [jnp.where(rclamp, u, a) for u, a in zip(here, right)]
            pairs = [d + r for d, r in zip(here[1:] + [bottom], beyond)]
            for i, y in enumerate(ys):
                at = (y, slice(j * 8, (j + 1) * 8), slice(None))
                new = af[at] * here[i] + cf[at] * (up_left[i] + pairs[i])
                dst[at] = jnp.where(active, new, here[i])
            left, here = here, right
        return carry

    lax.fori_loop(0, ROWS // block, body, 0)


def kernel(
    alpha_hbm, perturb_hbm, gain_hbm, bands_hbm, steps_hbm, out_ref,
    alpha_ref, perturb_ref, gain_ref, bands_ref, steps_ref,
    whi, wlo, vext, sib, hsend, hrecv, ub0, ub1, cf, af, gt, pf, pt, psend, smo, xs, xq, xpeak, xr, xscale, acc, zs, zr,
    in_sem, relay, hs_sem, hr_sem, ps_sem, pr_sem, xs_sem, xr_sem, zs_sem, zr_sem,
):
    h = lax.axis_index("lat")
    g = lax.axis_index("lon")
    mi = lax.axis_index("mem")
    z = mi // NX
    x = mi % NX
    oh = 1 - h
    gl = lax.rem(g + LON - 1, LON)
    gr = lax.rem(g + 1, LON)

    def xmem(d):
        return z * NX + lax.rem(x + d, NX)

    def zmem(d):
        return lax.rem(z + d, NZ) * NX + x

    partners = [(oh, g, mi)]
    partners += [(a, b, mi) for a in (h, oh) for b in (gl, gr)]
    ring = [(h, g, zmem(1)), (h, g, zmem(NZ - 1)), (h, g, xmem(1)), (h, g, xmem(NX - 1))]
    partners += ring
    barrier = pltpu.get_barrier_semaphore()
    for p in partners:
        pl.semaphore_signal(barrier, inc=1, device_id=p, device_id_type=pl.DeviceIdType.MESH)

    loads = [
        pltpu.make_async_copy(bands_hbm, bands_ref, in_sem.at[0]),
        pltpu.make_async_copy(steps_hbm, steps_ref, in_sem.at[1]),
    ]
    for i in range(4):
        part = pl.ds(i * 512, 512)
        loads.append(pltpu.make_async_copy(alpha_hbm.at[part], alpha_ref.at[part], in_sem.at[2 + i]))
    loads.append(pltpu.make_async_copy(gain_hbm, gain_ref, in_sem.at[6]))
    loads.append(pltpu.make_async_copy(perturb_hbm, perturb_ref, in_sem.at[7]))
    for cp in loads:
        cp.start()

    def relay_send(r):
        for i in range(4 if r == 1 else 2):
            pl.semaphore_signal(
                relay.at[r - 1, i], inc=1, device_id=ring[i], device_id_type=pl.DeviceIdType.MESH
            )

    def relay_wait(r):
        for i in range(4 if r == 1 else 2):
            pl.semaphore_wait(relay.at[r - 1, i], 1)

    def remote(src, dst, ssem, rsem, dev):
        return pltpu.make_async_remote_copy(
            src_ref=src, dst_ref=dst, send_sem=ssem, recv_sem=rsem,
            device_id=dev, device_id_type=pl.DeviceIdType.MESH,
        )

    loads[0].wait()
    loads[1].wait()
    n = iota((128, 256), 1)
    k = iota((128, 256), 0)
    core = lax.rem(h + n // 128, 2)
    member = lax.rem(n // 64, 2)
    q = lax.rem(n, 64)
    level = lax.rem(q, 8) * 16 + (q // 16) * 4 + core * 2 + lax.rem(q // 8, 2)
    onehot = jnp.where(k == level, 1.0, 0.0).astype(BF16)
    r8 = iota((8, 128), 0)
    rows = jnp.where(
        r8 == 0,
        jnp.broadcast_to(bands_ref[...].astype(F32), (8, 128)),
        jnp.broadcast_to(steps_ref[...].astype(F32), (8, 128)),
    ).astype(BF16)
    permuted = dot(rows, onehot)
    width = jnp.broadcast_to(permuted[0:1, :], (128, 256))
    count = jnp.broadcast_to(permuted[1:2, 0:128], (8, 128))
    distance = jnp.abs(k - level).astype(F32)
    raw = jnp.where(distance <= width, 1.0 - distance / (width + 1.0), 0.0)
    weights = raw / jnp.sum(raw, axis=0, keepdims=True)
    for m in range(2):
        high, low = split2(jnp.where(member == m, weights, 0.0))
        whi[m * 128 : (m + 1) * 128, :] = high
        wlo[m * 128 : (m + 1) * 128, :] = low

    def vertical(p, carry):
        turned = []
        for i in range(2):
            y = 2 * p + i
            a0 = alpha_ref[pl.ds(y, 128, stride=16), :]
            a1 = alpha_ref[pl.ds(y + 8, 128, stride=16), :]
            turned.append(jnp.concatenate([a0.T, a1.T], axis=1))
        high, low = split2(jnp.concatenate(turned, axis=0))
        w = whi[...]
        v = dot(high, w) + dot(low, w) + dot(high, wlo[...])
        for i in range(2):
            vext[h * 8 + 2 * p + i, HALO : HALO + TILE, :] = v[i * TILE : (i + 1) * TILE, 0:128]
            sib[2 * p + i] = v[i * TILE : (i + 1) * TILE, 128:256]
        for core in range(2):
            c = v[:, core * 128 : (core + 1) * 128]
            for side, x0 in enumerate((0, TILE - HALO)):
                hsend[core, side, p] = jnp.concatenate(
                    [c[x0 : x0 + HALO], c[TILE + x0 : TILE + x0 + HALO]], axis=0
                ).astype(BF16)
        return carry

    for cp in loads[2:6]:
        cp.wait()
    halo_copies = []
    for b in range(2):
        lax.fori_loop(2 * b, 2 * b + 2, vertical, 0)
        if b == 0:
            pl.semaphore_wait(barrier, len(partners))
            relay_send(1)
        own_pairs = pl.ds(h * 4 + 2 * b, 2)
        pairs = pl.ds(2 * b, 2)
        sends = [
            (hsend.at[0, 0, pairs], hrecv.at[1, own_pairs], (h, gl, mi)),
            (hsend.at[0, 1, pairs], hrecv.at[0, own_pairs], (h, gr, mi)),
            (hsend.at[1, 0, pairs], hrecv.at[1, own_pairs], (oh, gl, mi)),
            (hsend.at[1, 1, pairs], hrecv.at[0, own_pairs], (oh, gr, mi)),
            (sib.at[pl.ds(4 * b, 4)], vext.at[pl.ds(h * 8 + 4 * b, 4), pl.ds(HALO, TILE)], (oh, g, mi)),
        ]
        for i, (src, dst, dev) in enumerate(sends):
            cp = remote(src, dst, hs_sem.at[b, i], hr_sem.at[b, i], dev)
            cp.start()
            halo_copies.append(cp)

    def widen(i, carry):
        at = pl.ds(pl.multiple_of(i * 256, 256), 256)
        pf[at, :] = perturb_ref[at, :].astype(F32)
        return carry

    loads[7].wait()
    lax.fori_loop(0, 8, widen, 0)

    def pick(y, c):
        parts = []
        for m in range(2):
            for xx in range(NX):
                for lv in range(2):
                    parts.append(pf[pl.ds(xx * 64 + c * 32 + lv * 16 + m * 8 + y, 8, stride=256), :])
        return jnp.concatenate(parts, axis=0).astype(BF16)

    def pick_other(y, carry):
        psend[y] = pick(y, oh)
        return carry

    def pick_own(y, carry):
        pt[h * 8 + y] = pick(y, h)
        return carry

    lax.fori_loop(0, 8, pick_other, 0)
    pcopy = remote(psend, pt.at[pl.ds(h * 8, 8)], ps_sem.at[0], pr_sem.at[0], (oh, g, mi))
    pcopy.start()
    lax.fori_loop(0, 8, pick_own, 0)

    loads[6].wait()
    def gain_tile(t):
        tile = gain_ref[:, pl.ds(pl.multiple_of(t * TILE, TILE), TILE)]
        return (0.24 * jnp.concatenate([tile, jnp.zeros((TILE - ROWS, TILE), F32)], axis=0)).T

    gt[0:HALO, :] = gain_tile(gl)[TILE - HALO :, :]
    gt[HALO : HALO + TILE, :] = gain_tile(g)
    gt[HALO + TILE :, :] = gain_tile(gr)[:HALO, :]

    def spread(i, carry):
        for k in range(2):
            j = 2 * i + k
            columns = gt[pl.ds(j, 8, stride=NJ), :]
            at = pl.ds(pl.multiple_of(j * 8, 8), 8)
            for y in range(ROWS):
                c = jnp.broadcast_to(columns[:, y : y + 1], (8, 128))
                cf[y, at, :] = c
                af[y, at, :] = 1.0 - 4.0 * c
        return carry

    lax.fori_loop(0, NJ // 2, spread, 0)

    relay_wait(1)
    relay_send(2)
    for cp in halo_copies:
        cp.wait_recv()

    def restride(p, carry):
        lefts = hrecv[0, p].astype(F32)
        rights = hrecv[1, p].astype(F32)
        for i in range(2):
            y = 2 * p + i
            vext[y, 0:HALO, :] = lefts[i * HALO : (i + 1) * HALO]
            vext[y, HALO + TILE :, :] = rights[i * HALO : (i + 1) * HALO]
            for j in range(NJ):
                ub0[y, j * 8 : (j + 1) * 8, :] = vext[y, pl.ds(j, 8, stride=NJ), :]
        return carry

    lax.fori_loop(0, ROWS // 2, restride, 0)

    relay_wait(2)
    relay_send(3)
    sub = iota((8, 128), 0)
    lclamp = jnp.logical_and(sub == HALO // NJ, g == 0)
    rclamp = jnp.logical_and(sub == (HALO + TILE - 1) // NJ, g == LON - 1)

    def two_steps(s, carry):
        t = (2 * s).astype(F32)
        diffuse_step(ub0, ub1, cf, af, t < count, lclamp, rclamp, 8)
        diffuse_step(ub1, ub0, cf, af, t + 1.0 < count, lclamp, rclamp, 8)
        return carry

    lax.fori_loop(0, MAX_STEPS // 4, two_steps, 0)
    relay_wait(3)
    relay_send(4)
    lax.fori_loop(MAX_STEPS // 4, MAX_STEPS // 2, two_steps, 0)
    relay_wait(4)

    pcopy.wait_recv()

    xcopies = []
    for e in (1, 0):
        base = 8 * lax.rem(h + e, 2)

        def weigh(i, carry):
            for k in range(4):
                y = base + 4 * i + k
                for j in range(NJ):
                    smo[k, pl.ds(j, 8, stride=NJ), :] = ub0[y, j * 8 : (j + 1) * 8, :]
            for k in range(4):
                row = 4 * i + k
                y = base + row
                product = smo[k, HALO : HALO + TILE, :].T * pt[y].astype(F32)
                total = (product[0:64, :] + product[64:128, :]) * 0.125
                for xx in range(NX):
                    part = total[xx * 16 : (xx + 1) * 16, :]
                    xs[xx, y] = part
                    xpeak[xx, pl.ds(row, 1), :] = jnp.max(jnp.abs(part), axis=0, keepdims=True)
            return carry

        lax.fori_loop(0, 2, weigh, 0)
        group = []
        for d in (2, 1, 3):
            t = lax.rem(x + d, NX)
            code = jnp.ceil(jnp.log2(jnp.maximum(xpeak[t], 1e-30)) * 256.0) + 1.0
            inverse = 32700.0 / jnp.exp2(code * (1.0 / 256.0))
            for row in range(8):
                part = xs[t, base + row] * inverse[row : row + 1, :]
                xq[d - 1, e, row] = jnp.round(part).astype(jnp.int32).astype(jnp.int16)
            codes = jnp.concatenate([code, code], axis=0)
            xq[d - 1, e, 8] = codes.astype(jnp.int32).astype(jnp.int16)
            cp = remote(
                xq.at[d - 1, e], xr.at[d - 1, e],
                xs_sem.at[e, d - 1], xr_sem.at[e, d - 1], (h, g, xmem(d)),
            )
            cp.start()
            group.append(cp)
        xcopies.append(group)

    zcopies = []
    for e, group in zip((1, 0), xcopies):
        to = lax.rem(h + e, 2)
        base = 8 * to
        for cp in group:
            cp.wait_recv()

        for d in range(NX - 1):
            codes = xr[d, e, 8].astype(jnp.int32).astype(F32)[0:8]
            xscale[d] = jnp.exp2(codes * (1.0 / 256.0)) * (1.0 / 32700.0)

        def gather(i, carry):
            y = base + i
            total = xs[x, y]
            for d in range(NX - 1):
                total = total + xr[d, e, i].astype(jnp.int32).astype(F32) * xscale[d, pl.ds(i, 1), :]
            acc[pl.ds(pl.multiple_of(y * 16, 16), 16), :] = total
            return carry

        lax.fori_loop(0, 8, gather, 0)
        for zz in range(NZ):
            for lv in range(2):
                zs[zz, e, lv] = acc[pl.ds(to * 128 + lv * 8 + zz, 8, stride=16), :]
        for d in (4, 3, 5, 2, 6, 1, 7, 0):
            if d == 0 and e == 0:
                continue
            cp = remote(
                zs.at[lax.rem(z + d, NZ), e], zr.at[d * 2 + e],
                zs_sem.at[d * 2 + e], zr_sem.at[d * 2 + e], (to, g, zmem(d)),
            )
            cp.start()
            zcopies.append(cp)
    for cp in zcopies:
        cp.wait_recv()
    same = zs[z, 0]
    other = zr[1]
    for d in range(1, NZ):
        same = same + zr[2 * d]
        other = other + zr[2 * d + 1]
    out_ref[pl.ds(2 * h, 2)] = same
    out_ref[pl.ds(2 * oh, 2)] = other

    for cp in halo_copies + [pcopy] + xcopies[0] + xcopies[1] + zcopies:
        cp.wait_send()


def body(alpha, perturb, smooth_gain, bands, steps):
    vmem = pl.BlockSpec(memory_space=pltpu.VMEM)
    dma = pltpu.SemaphoreType.DMA
    return pl.pallas_call(
        kernel,
        out_shape=jax.ShapeDtypeStruct((4, 8, TILE), F32),
        in_specs=[pl.BlockSpec(memory_space=pl.ANY)] * 5,
        out_specs=vmem,
        scratch_shapes=[
            pltpu.VMEM((2048, TILE), F32),
            pltpu.VMEM((2048, TILE), BF16),
            pltpu.VMEM((ROWS, LON * TILE), F32),
            pltpu.VMEM((1, 128), jnp.int32),
            pltpu.VMEM((1, 128), jnp.int32),
            pltpu.VMEM((256, 256), BF16),
            pltpu.VMEM((256, 256), BF16),
            pltpu.VMEM((ROWS, EXT, 128), F32),
            pltpu.VMEM((8, TILE, 128), F32),
            pltpu.VMEM((2, 2, 4, 2 * HALO, 128), BF16),
            pltpu.VMEM((2, ROWS // 2, 2 * HALO, 128), BF16),
            pltpu.VMEM((ROWS, EXT, 128), F32),
            pltpu.VMEM((ROWS, EXT, 128), F32),
            pltpu.VMEM((ROWS, EXT, 128), F32),
            pltpu.VMEM((ROWS, EXT, 128), F32),
            pltpu.VMEM((EXT, 128), F32),
            pltpu.VMEM((2048, 128), F32),
            pltpu.VMEM((ROWS, 128, TILE), BF16),
            pltpu.VMEM((8, 128, TILE), BF16),
            pltpu.VMEM((4, EXT, 128), F32),
            pltpu.VMEM((NX, ROWS, 16, TILE), F32),
            pltpu.VMEM((NX - 1, 2, 9, 16, TILE), jnp.int16),
            pltpu.VMEM((NX, 8, TILE), F32),
            pltpu.VMEM((NX - 1, 2, 9, 16, TILE), jnp.int16),
            pltpu.VMEM((NX - 1, 8, TILE), F32),
            pltpu.VMEM((256, TILE), F32),
            pltpu.VMEM((NZ, 2, 2, 8, TILE), F32),
            pltpu.VMEM((2 * NZ, 2, 8, TILE), F32),
            dma((8,)), pltpu.SemaphoreType.REGULAR((4, 4)), dma((2, 5)), dma((2, 5)), dma((1,)), dma((1,)),
            dma((2, 3)), dma((2, 3)), dma((16,)), dma((16,)),
        ],
        compiler_params=pltpu.CompilerParams(
            collective_id=0, has_side_effects=True, vmem_limit_bytes=60 << 20
        ),
    )(
        alpha.reshape(2048, TILE),
        perturb.reshape(2048, TILE),
        smooth_gain,
        bands.reshape(1, 128),
        steps.reshape(1, 128),
    )


def solution(mesh):
    placed = (P(None, "mem", "lat", "lon"), P(None, "mem", "lat", "lon"), P(), P(), P())
    return jax.shard_map(
        body, mesh=mesh, in_specs=placed, out_specs=P("mem", "lat", "lon"), check_vma=False
    )
```

```python
import jax
import jax.numpy as jnp
from jax import lax
from jax.experimental import pallas as pl
from jax.experimental.pallas import tpu as pltpu
from jax.sharding import PartitionSpec as P

F32 = jnp.float32
BF16 = jnp.bfloat16
HALO = 24
TILE = 128
EXT = TILE + 2 * HALO
NJ = EXT // 8
PAD = EXT + 24
ROWS = 16
MAX_STEPS = 24
NX = 4
NZ = 8
LON = 8


def iota(shape, dim):
    return lax.broadcasted_iota(jnp.int32, shape, dim)


def split2(value):
    high = value.astype(BF16)
    low = (value - high.astype(F32)).astype(BF16)
    return high, low


def dot(a, b):
    return jnp.dot(a, b, preferred_element_type=F32)


def diffuse_step(src, dst, cf, af, active, lclamp, rclamp, block):
    def body(b, carry):
        y0 = b * block
        above = jnp.maximum(y0 - 1, 0)
        below = jnp.minimum(y0 + block, ROWS - 1)
        ys = [y0 + i for i in range(block)]

        def load(y, j):
            return src[y, j * 8 : (j + 1) * 8, :]

        left = [pltpu.roll(load(y, NJ - 1), 1, 0) for y in ys]
        here = [load(y, 0) for y in ys]
        pairs = None
        for j in range(NJ):
            if j < NJ - 1:
                right = [load(y, j + 1) for y in ys]
            else:
                right = [pltpu.roll(load(y, 0), 7, 0) for y in ys]
            top, bottom = load(above, j), load(below, j)
            if j == HALO % NJ:
                left = [jnp.where(lclamp, u, a) for u, a in zip(here, left)]
            if pairs is None or j == HALO % NJ:
                up_left = [u + a for u, a in zip([top] + here[:-1], left)]
            else:
                up_left = [top + left[0]] + pairs[:-1]
            beyond = right
            if j == (HALO + TILE - 1) % NJ:
                beyond = [jnp.where(rclamp, u, a) for u, a in zip(here, right)]
            pairs = [d + r for d, r in zip(here[1:] + [bottom], beyond)]
            for i, y in enumerate(ys):
                at = (y, slice(j * 8, (j + 1) * 8), slice(None))
                new = af[at] * here[i] + cf[at] * (up_left[i] + pairs[i])
                dst[at] = jnp.where(active, new, here[i])
            left, here = here, right
        return carry

    lax.fori_loop(0, ROWS // block, body, 0)


def kernel(
    alpha_hbm, perturb_hbm, gain_hbm, bands_hbm, steps_hbm, out_ref,
    alpha_ref, perturb_ref, gain_ref, bands_ref, steps_ref,
    whi, wlo, vext, sib, hsend, hrecv, ub0, ub1, cf, af, gt, pf, pt, psend, smo, xs, xq, xpeak, xr, xscale, acc, zs, zr,
    in_sem, relay, hs_sem, hr_sem, ps_sem, pr_sem, xs_sem, xr_sem, zs_sem, zr_sem,
):
    h = lax.axis_index("lat")
    g = lax.axis_index("lon")
    mi = lax.axis_index("mem")
    z = mi // NX
    x = mi % NX
    oh = 1 - h
    gl = lax.rem(g + LON - 1, LON)
    gr = lax.rem(g + 1, LON)

    def xmem(d):
        return z * NX + lax.rem(x + d, NX)

    def zmem(d):
        return lax.rem(z + d, NZ) * NX + x

    partners = [(oh, g, mi)]
    partners += [(a, b, mi) for a in (h, oh) for b in (gl, gr)]
    ring = [(h, g, zmem(1)), (h, g, zmem(NZ - 1)), (h, g, xmem(1)), (h, g, xmem(NX - 1))]
    partners += ring
    barrier = pltpu.get_barrier_semaphore()
    for p in partners:
        pl.semaphore_signal(barrier, inc=1, device_id=p, device_id_type=pl.DeviceIdType.MESH)

    loads = [
        pltpu.make_async_copy(bands_hbm, bands_ref, in_sem.at[0]),
        pltpu.make_async_copy(steps_hbm, steps_ref, in_sem.at[1]),
    ]
    for i in range(4):
        part = pl.ds(i * 512, 512)
        loads.append(pltpu.make_async_copy(alpha_hbm.at[part], alpha_ref.at[part], in_sem.at[2 + i]))
    loads.append(pltpu.make_async_copy(gain_hbm, gain_ref, in_sem.at[6]))
    loads.append(pltpu.make_async_copy(perturb_hbm, perturb_ref, in_sem.at[7]))
    for cp in loads:
        cp.start()

    def relay_send(r):
        for i in range(4 if r == 1 else 2):
            pl.semaphore_signal(
                relay.at[r - 1, i], inc=1, device_id=ring[i], device_id_type=pl.DeviceIdType.MESH
            )

    def relay_wait(r):
        for i in range(4 if r == 1 else 2):
            pl.semaphore_wait(relay.at[r - 1, i], 1)

    def remote(src, dst, ssem, rsem, dev):
        return pltpu.make_async_remote_copy(
            src_ref=src, dst_ref=dst, send_sem=ssem, recv_sem=rsem,
            device_id=dev, device_id_type=pl.DeviceIdType.MESH,
        )

    loads[0].wait()
    loads[1].wait()
    n = iota((128, 256), 1)
    k = iota((128, 256), 0)
    core = lax.rem(h + n // 128, 2)
    member = lax.rem(n // 64, 2)
    q = lax.rem(n, 64)
    level = lax.rem(q, 8) * 16 + (q // 16) * 4 + core * 2 + lax.rem(q // 8, 2)
    onehot = jnp.where(k == level, 1.0, 0.0).astype(BF16)
    r8 = iota((8, 128), 0)
    rows = jnp.where(
        r8 == 0,
        jnp.broadcast_to(bands_ref[...].astype(F32), (8, 128)),
        jnp.broadcast_to(steps_ref[...].astype(F32), (8, 128)),
    ).astype(BF16)
    permuted = dot(rows, onehot)
    width = jnp.broadcast_to(permuted[0:1, :], (128, 256))
    count = jnp.broadcast_to(permuted[1:2, 0:128], (8, 128))
    distance = jnp.abs(k - level).astype(F32)
    raw = jnp.where(distance <= width, 1.0 - distance / (width + 1.0), 0.0)
    weights = raw / jnp.sum(raw, axis=0, keepdims=True)
    for m in range(2):
        high, low = split2(jnp.where(member == m, weights, 0.0))
        whi[m * 128 : (m + 1) * 128, :] = high
        wlo[m * 128 : (m + 1) * 128, :] = low

    def vertical(p, carry):
        turned = []
        for i in range(2):
            y = 2 * p + i
            a0 = alpha_ref[pl.ds(y, 128, stride=16), :]
            a1 = alpha_ref[pl.ds(y + 8, 128, stride=16), :]
            turned.append(jnp.concatenate([a0.T, a1.T], axis=1))
        high, low = split2(jnp.concatenate(turned, axis=0))
        w = whi[...]
        v = dot(high, w) + dot(low, w) + dot(high, wlo[...])
        for i in range(2):
            vext[h * 8 + 2 * p + i, HALO : HALO + TILE, :] = v[i * TILE : (i + 1) * TILE, 0:128]
            sib[2 * p + i] = v[i * TILE : (i + 1) * TILE, 128:256]
        for core in range(2):
            c = v[:, core * 128 : (core + 1) * 128]
            for side, x0 in enumerate((0, TILE - HALO)):
                hsend[core, side, p] = jnp.concatenate(
                    [c[x0 : x0 + HALO], c[TILE + x0 : TILE + x0 + HALO]], axis=0
                ).astype(BF16)
        return carry

    for cp in loads[2:6]:
        cp.wait()
    halo_copies = []
    for b in range(2):
        lax.fori_loop(2 * b, 2 * b + 2, vertical, 0)
        if b == 0:
            pl.semaphore_wait(barrier, len(partners))
            relay_send(1)
        own_pairs = pl.ds(h * 4 + 2 * b, 2)
        pairs = pl.ds(2 * b, 2)
        sends = [
            (hsend.at[0, 0, pairs], hrecv.at[1, own_pairs], (h, gl, mi)),
            (hsend.at[0, 1, pairs], hrecv.at[0, own_pairs], (h, gr, mi)),
            (hsend.at[1, 0, pairs], hrecv.at[1, own_pairs], (oh, gl, mi)),
            (hsend.at[1, 1, pairs], hrecv.at[0, own_pairs], (oh, gr, mi)),
            (sib.at[pl.ds(4 * b, 4)], vext.at[pl.ds(h * 8 + 4 * b, 4), pl.ds(HALO, TILE)], (oh, g, mi)),
        ]
        for i, (src, dst, dev) in enumerate(sends):
            cp = remote(src, dst, hs_sem.at[b, i], hr_sem.at[b, i], dev)
            cp.start()
            halo_copies.append(cp)

    def widen(i, carry):
        at = pl.ds(pl.multiple_of(i * 256, 256), 256)
        pf[at, :] = perturb_ref[at, :].astype(F32)
        return carry

    loads[7].wait()
    lax.fori_loop(0, 8, widen, 0)

    def pick(y, c):
        parts = []
        for m in range(2):
            for xx in range(NX):
                for lv in range(2):
                    parts.append(pf[pl.ds(xx * 64 + c * 32 + lv * 16 + m * 8 + y, 8, stride=256), :])
        return jnp.concatenate(parts, axis=0).astype(BF16)

    def pick_other(y, carry):
        psend[y] = pick(y, oh)
        return carry

    def pick_own(y, carry):
        pt[h * 8 + y] = pick(y, h)
        return carry

    lax.fori_loop(0, 8, pick_other, 0)
    pcopy = remote(psend, pt.at[pl.ds(h * 8, 8)], ps_sem.at[0], pr_sem.at[0], (oh, g, mi))
    pcopy.start()
    lax.fori_loop(0, 8, pick_own, 0)

    loads[6].wait()
    def gain_tile(t):
        tile = gain_ref[:, pl.ds(pl.multiple_of(t * TILE, TILE), TILE)]
        return (0.24 * jnp.concatenate([tile, jnp.zeros((TILE - ROWS, TILE), F32)], axis=0)).T

    gt[0:HALO, :] = gain_tile(gl)[TILE - HALO :, :]
    gt[HALO : HALO + TILE, :] = gain_tile(g)
    gt[HALO + TILE : EXT, :] = gain_tile(gr)[:HALO, :]

    def spread(i, carry):
        for k in range(2):
            j = 2 * i + k
            columns = gt[pl.ds(j, 8, stride=NJ), :]
            at = pl.ds(pl.multiple_of(j * 8, 8), 8)
            for y in range(ROWS):
                c = jnp.broadcast_to(columns[:, y : y + 1], (8, 128))
                cf[y, at, :] = c
                af[y, at, :] = 1.0 - 4.0 * c
        return carry

    lax.fori_loop(0, NJ // 2, spread, 0)

    relay_wait(1)
    relay_send(2)
    for cp in halo_copies:
        cp.wait_recv()

    def restride(p, carry):
        lefts = hrecv[0, p].astype(F32)
        rights = hrecv[1, p].astype(F32)
        for i in range(2):
            y = 2 * p + i
            vext[y, 0:HALO, :] = lefts[i * HALO : (i + 1) * HALO]
            vext[y, HALO + TILE : EXT, :] = rights[i * HALO : (i + 1) * HALO]
            for j in range(NJ):
                ub0[y, j * 8 : (j + 1) * 8, :] = vext[y, pl.ds(j, 8, stride=NJ), :]
        return carry

    lax.fori_loop(0, ROWS // 2, restride, 0)

    relay_wait(2)
    relay_send(3)
    sub = iota((8, 128), 0)
    lclamp = jnp.logical_and(sub == HALO // NJ, g == 0)
    rclamp = jnp.logical_and(sub == (HALO + TILE - 1) // NJ, g == LON - 1)

    def two_steps(s, carry):
        t = (2 * s).astype(F32)
        diffuse_step(ub0, ub1, cf, af, t < count, lclamp, rclamp, 8)
        diffuse_step(ub1, ub0, cf, af, t + 1.0 < count, lclamp, rclamp, 8)
        return carry

    lax.fori_loop(0, MAX_STEPS // 4, two_steps, 0)
    relay_wait(3)
    relay_send(4)
    lax.fori_loop(MAX_STEPS // 4, MAX_STEPS // 2, two_steps, 0)
    relay_wait(4)

    pcopy.wait_recv()

    xcopies = []
    for e in (1, 0):
        base = 8 * lax.rem(h + e, 2)

        def weigh(i, carry):
            for k in range(4):
                y = base + 4 * i + k
                for j in range(NJ):
                    smo[k, pl.ds(j, 8, stride=NJ), :] = ub0[y, j * 8 : (j + 1) * 8, :]
            for k in range(4):
                row = 4 * i + k
                y = base + row
                product = smo[k, HALO : HALO + TILE, :].T * pt[y].astype(F32)
                total = (product[0:64, :] + product[64:128, :]) * 0.125
                for xx in range(NX):
                    part = total[xx * 16 : (xx + 1) * 16, :]
                    xs[xx, y] = part
                    xpeak[xx, pl.ds(row, 1), :] = jnp.max(jnp.abs(part), axis=0, keepdims=True)
            return carry

        lax.fori_loop(0, 2, weigh, 0)
        group = []
        for d in (2, 1, 3):
            t = lax.rem(x + d, NX)
            code = jnp.ceil(jnp.log2(jnp.maximum(xpeak[t], 1e-30)) * 256.0) + 1.0
            inverse = 32700.0 / jnp.exp2(code * (1.0 / 256.0))
            for row in range(8):
                part = xs[t, base + row] * inverse[row : row + 1, :]
                xq[d - 1, e, row] = jnp.round(part).astype(jnp.int32).astype(jnp.int16)
            codes = jnp.concatenate([code, code], axis=0)
            xq[d - 1, e, 8] = codes.astype(jnp.int32).astype(jnp.int16)
            cp = remote(
                xq.at[d - 1, e], xr.at[d - 1, e],
                xs_sem.at[e, d - 1], xr_sem.at[e, d - 1], (h, g, xmem(d)),
            )
            cp.start()
            group.append(cp)
        xcopies.append(group)

    zcopies = []
    for e, group in zip((1, 0), xcopies):
        to = lax.rem(h + e, 2)
        base = 8 * to
        for cp in group:
            cp.wait_recv()

        for d in range(NX - 1):
            codes = xr[d, e, 8].astype(jnp.int32).astype(F32)[0:8]
            xscale[d] = jnp.exp2(codes * (1.0 / 256.0)) * (1.0 / 32700.0)

        def gather(i, carry):
            y = base + i
            total = xs[x, y]
            for d in range(NX - 1):
                total = total + xr[d, e, i].astype(jnp.int32).astype(F32) * xscale[d, pl.ds(i, 1), :]
            acc[pl.ds(pl.multiple_of(y * 16, 16), 16), :] = total
            return carry

        lax.fori_loop(0, 8, gather, 0)
        for zz in range(NZ):
            for lv in range(2):
                zs[zz, e, lv] = acc[pl.ds(to * 128 + lv * 8 + zz, 8, stride=16), :]
        for d in (4, 3, 5, 2, 6, 1, 7, 0):
            if d == 0 and e == 0:
                continue
            cp = remote(
                zs.at[lax.rem(z + d, NZ), e], zr.at[d * 2 + e],
                zs_sem.at[d * 2 + e], zr_sem.at[d * 2 + e], (to, g, zmem(d)),
            )
            cp.start()
            zcopies.append(cp)
    for cp in zcopies:
        cp.wait_recv()
    same = zs[z, 0]
    other = zr[1]
    for d in range(1, NZ):
        same = same + zr[2 * d]
        other = other + zr[2 * d + 1]
    out_ref[pl.ds(2 * h, 2)] = same
    out_ref[pl.ds(2 * oh, 2)] = other

    for cp in halo_copies + [pcopy] + xcopies[0] + xcopies[1] + zcopies:
        cp.wait_send()


def body(alpha, perturb, smooth_gain, bands, steps):
    vmem = pl.BlockSpec(memory_space=pltpu.VMEM)
    dma = pltpu.SemaphoreType.DMA
    return pl.pallas_call(
        kernel,
        out_shape=jax.ShapeDtypeStruct((4, 8, TILE), F32),
        in_specs=[pl.BlockSpec(memory_space=pl.ANY)] * 5,
        out_specs=vmem,
        scratch_shapes=[
            pltpu.VMEM((2048 + 16, TILE), F32),
            pltpu.VMEM((2048, TILE), BF16),
            pltpu.VMEM((ROWS, LON * TILE), F32),
            pltpu.VMEM((1, 128), jnp.int32),
            pltpu.VMEM((1, 128), jnp.int32),
            pltpu.VMEM((256, 256), BF16),
            pltpu.VMEM((256, 256), BF16),
            pltpu.VMEM((ROWS, PAD, 128), F32),
            pltpu.VMEM((8, TILE, 128), F32),
            pltpu.VMEM((2, 2, 4, 2 * HALO, 128), BF16),
            pltpu.VMEM((2, ROWS // 2, 2 * HALO, 128), BF16),
            pltpu.VMEM((ROWS, EXT, 128), F32),
            pltpu.VMEM((ROWS, EXT, 128), F32),
            pltpu.VMEM((ROWS, EXT, 128), F32),
            pltpu.VMEM((ROWS, EXT, 128), F32),
            pltpu.VMEM((PAD, 128), F32),
            pltpu.VMEM((2048 + 256, 128), F32),
            pltpu.VMEM((ROWS, 128, TILE), BF16),
            pltpu.VMEM((8, 128, TILE), BF16),
            pltpu.VMEM((4, PAD, 128), F32),
            pltpu.VMEM((NX, ROWS, 16, TILE), F32),
            pltpu.VMEM((NX - 1, 2, 9, 16, TILE), jnp.int16),
            pltpu.VMEM((NX, 8, TILE), F32),
            pltpu.VMEM((NX - 1, 2, 9, 16, TILE), jnp.int16),
            pltpu.VMEM((NX - 1, 8, TILE), F32),
            pltpu.VMEM((256 + 16, TILE), F32),
            pltpu.VMEM((NZ, 2, 2, 8, TILE), F32),
            pltpu.VMEM((2 * NZ, 2, 8, TILE), F32),
            dma((8,)), pltpu.SemaphoreType.REGULAR((4, 4)), dma((2, 5)), dma((2, 5)), dma((1,)), dma((1,)),
            dma((2, 3)), dma((2, 3)), dma((16,)), dma((16,)),
        ],
        compiler_params=pltpu.CompilerParams(
            collective_id=0, has_side_effects=True, vmem_limit_bytes=60 << 20
        ),
    )(
        alpha.reshape(2048, TILE),
        perturb.reshape(2048, TILE),
        smooth_gain,
        bands.reshape(1, 128),
        steps.reshape(1, 128),
    )


def solution(mesh):
    placed = (P(None, "mem", "lat", "lon"), P(None, "mem", "lat", "lon"), P(), P(), P())
    return jax.shard_map(
        body, mesh=mesh, in_specs=placed, out_specs=P("mem", "lat", "lon"), check_vma=False
    )
```
